128 devices in a mesh: pulse: 16 (over y, z), tile: 4 (over x), band: 2 (over core).
Axes of the slice: x: 4, y: 4, z: 4, core: 2. Of those that a mesh axis runs over, the one named last changes fastest.
Arguments:
- echo: bfloat16 [2, 16, 16384], P(None, 'pulse', 'band'), may hold values from -6 to 6
- offsets: int32 [16, 32, 4096], P('pulse', 'tile'), may hold values from 0 to 8184
- delta: float32 [16], P('pulse'), may hold values from -3 to 3
- look: float32 [16, 4096], P('pulse'), may hold values from 0.5 to 1.5
Outputs:
- image: float32 [2, 32, 4096], P(None, 'tile', 'pulse')
- focus_gradient: float32 [16], P('pulse')
The draws below stay inside these ranges and needn't reach their ends.
All inputs are finite; a program needn't handle non-finite values.
Results may differ from the reference program's by a relative error of at most 0.0003.
Values sent between devices are 32-bit elements; how exact they have to be, the bound alone decides.
No kernel may reach another device: no remote copies, remote signals or barrier semaphores. Data moves between devices by JAX's collectives and lax.ppermute only.
A program may use at most 64 MiB of HBM per device.

```python
import math
import jax
import jax.numpy as jnp
from jax import lax

COLS = 4096
BINS = 8192
PULSES = 16
ROWS = 32
RANGE = 16384
N_BAND = 2


def plant(entries, key, low, top_value):
    extent = entries.shape
    spot = [jax.random.randint(jax.random.fold_in(key, axis), (), 0, extent[axis]) for axis in range(len(extent))]
    entries = entries.at[tuple(spot)].set(low)
    longest = extent.index(max(extent))
    spot[longest] = (spot[longest] + 1) % extent[longest]
    return entries.at[tuple(spot)].set(top_value)


def block_levels(key, shape, cuts, low, largest):
    def one(dim, shards_of):
        steps = jax.random.uniform(jax.random.fold_in(jax.random.fold_in(key, 6), dim), (shards_of,), jnp.float32, low / len(cuts), largest / len(cuts))
        return jnp.repeat(jnp.exp(steps), shape[dim] // shards_of).reshape((-1,) + (1,) * (len(shape) - dim - 1))

    loudness = one(*cuts[0])
    for cut in cuts[1:]:
        loudness = loudness * one(*cut)
    return loudness


def bell_draw(key, shape, spread, bound, pieces=(), held_as=jnp.bfloat16):
    loudness = block_levels(key, shape, pieces, -0.22, 0.18) if pieces else 1.0
    array = jax.random.normal(key, shape, jnp.float32) * spread * loudness
    return jnp.minimum(jnp.maximum(array, -bound), bound).astype(held_as)


def setup_inputs(seed: int = 0) -> dict:
    arg_keys = jax.random.split(jax.random.key(seed), 5)
    echo = bell_draw(arg_keys[0], (2, PULSES, RANGE), 1.0, 6.0, ((1, 16), (2, 2)))
    offsets = plant(jax.random.randint(arg_keys[1], (PULSES, ROWS, COLS), 0, BINS - 7), jax.random.fold_in(arg_keys[1], 1), 0, (BINS - 7) - 1).astype(jnp.int32)
    delta = bell_draw(arg_keys[2], (PULSES,), 0.5, 3.0, ((0, 16),), jnp.float32)
    look = jnp.clip(0.5 + 1.0 * jax.random.uniform(arg_keys[3], (PULSES, COLS), jnp.float32) ** block_levels(arg_keys[3], (PULSES, COLS), ((0, 16),), -0.2, 0.2), 0.5, 1.5)
    return {"echo": echo, "offsets": offsets, "delta": delta, "look": look}


filter_taps = (-0.0136, 0.0637, -0.1804, 0.6366, 0.6366, -0.1804, 0.0637, -0.0136)
power_floor = 1e-06

def filtered(echo_part):
    length = echo_part.shape[-1] - 7
    summed = filter_taps[0] * echo_part[..., 0:length].astype(jnp.float32)
    for lag_index in range(1, 8):
        summed = summed + filter_taps[lag_index] * echo_part[..., lag_index:lag_index + length].astype(jnp.float32)
    return summed

def pulse_terms(filt, offsets, delta, look, multiplier):
    flat = offsets.reshape(offsets.shape[0], -1)
    real_in = jnp.take_along_axis(filt[0], flat, axis=1).reshape(offsets.shape)
    imag_in = jnp.take_along_axis(filt[1], flat, axis=1).reshape(offsets.shape)
    phase_index = offsets * multiplier % 64
    angle = phase_index.astype(jnp.float32) * (math.pi / 32.0) + delta[:, None, None] * look[:, None, :]
    cosine = jnp.cos(angle)
    sine = jnp.sin(angle)
    return (cosine * real_in - sine * imag_in, sine * real_in + cosine * imag_in)

def reference(echo, offsets, delta, look):
    npix = ROWS * COLS
    image = jnp.zeros((2, ROWS, COLS), jnp.float32)
    filters = []
    for band_number in range(N_BAND):
        band_echo = echo[:, :, band_number * BINS:(band_number + 1) * BINS]
        filt = jnp.moveaxis(filtered(band_echo), 1, 0)
        filters.append(filt)
        multiplier = 5 + 2 * band_number

        def add_pulse(carry, inputs):
            filt_one, offs_one, delta_one, look_one = inputs
            real_t, imag_t = pulse_terms(filt_one[:, None, :], offs_one[None], delta_one[None], look_one[None], multiplier)
            return (carry + jnp.stack((real_t[0], imag_t[0])), None)
        image, unused = lax.scan(add_pulse, image, (filt, offsets, delta, look))
    power = image[0] * image[0] + image[1] * image[1]
    mean_power = jnp.sum(power) / npix + power_floor
    quart = jnp.sum(power * power) / npix
    weight = 2.0 * power / (mean_power * mean_power) - 2.0 * quart / (mean_power * mean_power * mean_power)
    adj_real = weight * image[0]
    adj_imag = weight * image[1]
    gradient = jnp.zeros((PULSES,), jnp.float32)
    for band_number in range(N_BAND):
        multiplier = 5 + 2 * band_number

        def pulse_grad(carry, inputs):
            filt_one, offs_one, delta_one, look_one = inputs
            real_t, imag_t = pulse_terms(filt_one[:, None, :], offs_one[None], delta_one[None], look_one[None], multiplier)
            value = jnp.sum(look_one[None, :] * (adj_imag * real_t[0] - adj_real * imag_t[0]))
            return (carry, value)
        unused, values = lax.scan(pulse_grad, jnp.float32(0.0), (filters[band_number], offsets, delta, look))
        gradient = gradient + values
    focus_gradient = math.sqrt(PULSES / npix) * gradient
    return (image, focus_gradient)
```

```python
import math

import jax
import jax.numpy as jnp
from jax import lax
from jax.experimental import pallas as pl
from jax.experimental.pallas import tpu as pltpu
from jax.sharding import PartitionSpec as P

filter_taps = (-0.0136, 0.0637, -0.1804, 0.6366, 0.6366, -0.1804, 0.0637, -0.0136)
power_floor = 1e-06

LANES = 128
ROWS_DEV = 8
GROUP = 2


def sine_cosine(angle):
    turns = jnp.floor(angle * (2.0 / math.pi) + 0.5)
    rest = angle - turns * 1.5703125
    rest = rest - turns * 4.837512969970703125e-4
    rest = rest - turns * 7.549789948768648e-8
    square = rest * rest
    sine = rest + rest * square * (
        -1.6666654611e-1 + square * (8.3321608736e-3 + square * -1.9515295891e-4)
    )
    cosine = 1.0 - 0.5 * square + square * square * (
        4.166664568298827e-2 + square * (-1.388731625493765e-3 + square * 2.443315711809948e-5)
    )
    quadrant = turns.astype(jnp.int32) & 3
    swap = (quadrant & 1) == 1
    sine_out = jnp.where(swap, cosine, sine)
    cosine_out = jnp.where(swap, sine, cosine)
    sine_out = jnp.where(quadrant >= 2, -sine_out, sine_out)
    cosine_out = jnp.where((quadrant == 1) | (quadrant == 2), -cosine_out, cosine_out)
    return sine_out, cosine_out


def filtered_rows(echo_rows):
    rows = echo_rows.shape[0]
    lane = lax.broadcasted_iota(jnp.int32, echo_rows.shape, 1)
    inside = filter_taps[0] * echo_rows
    across = jnp.zeros_like(echo_rows)
    for lag in range(1, 8):
        moved = filter_taps[lag] * pltpu.roll(echo_rows, LANES - lag, 1)
        here = lane < LANES - lag
        inside = inside + jnp.where(here, moved, 0.0)
        across = across + jnp.where(here, 0.0, moved)
    return inside + pltpu.roll(across, rows - 1, 0)


def lane_lookup(row, lanes):
    return jnp.take_along_axis(row, lanes, axis=1, mode="promise_in_bounds")


def terms_kernel(delta_ref, echo_ref, offsets_ref, look_ref, out_ref, table_ref, turn_ref):
    table_rows = table_ref.shape[1]
    blocks = out_ref.shape[0]
    multiplier = 5 + 2 * lax.axis_index("band")
    lane = lax.broadcasted_iota(jnp.int32, (1, LANES), 1)
    phase_index = (lane * multiplier) & 63
    sine, cosine = sine_cosine(phase_index.astype(jnp.float32) * (math.pi / 32.0))
    filt = []
    for part in range(2):
        rows = echo_ref[part].astype(jnp.float32).reshape(table_rows, LANES)
        filt.append(filtered_rows(rows))
    table_ref[0] = cosine * filt[0] - sine * filt[1]
    table_ref[1] = sine * filt[0] + cosine * filt[1]
    turn_sine, turn_cosine = sine_cosine(delta_ref[0] * look_ref[...])
    turn_ref[0] = turn_cosine
    turn_ref[1] = turn_sine

    def some_blocks(step, carry):
        starts = [pl.multiple_of((step * GROUP + j) * LANES, LANES) for j in range(GROUP)]
        offsets = [offsets_ref[0, :, pl.ds(start, LANES)] for start in starts]
        lanes = [k & (LANES - 1) for k in offsets]
        highs = [k >> 7 for k in offsets]
        bits = [[((high >> bit) & 1) == 1 for bit in range(6)] for high in highs]

        def select(first, level, part):
            if level == 0:
                row = jnp.broadcast_to(table_ref[part, pl.ds(first, 1), :], (ROWS_DEV, LANES))
                return [lane_lookup(row, lanes[j]) for j in range(GROUP)]
            low = select(first, level - 1, part)
            high = select(first + (1 << (level - 1)), level - 1, part)
            return [jnp.where(bits[j][level - 1], high[j], low[j]) for j in range(GROUP)]

        real_in = select(0, 6, 0)
        imag_in = select(0, 6, 1)
        for j in range(GROUP):
            cos_turn = turn_ref[0, :, pl.ds(starts[j], LANES)]
            sin_turn = turn_ref[1, :, pl.ds(starts[j], LANES)]
            out_ref[step * GROUP + j, 0] = cos_turn * real_in[j] - sin_turn * imag_in[j]
            out_ref[step * GROUP + j, 1] = sin_turn * real_in[j] + cos_turn * imag_in[j]
        return carry

    lax.fori_loop(0, blocks // GROUP, some_blocks, 0)


def image_kernel(terms_ref, image_ref, sums_ref):
    pulses = terms_ref.shape[0] // 2
    copies = sums_ref.shape[0] // pulses
    real_parts = []
    imag_parts = []
    for pulse in range(pulses):
        real_parts.append(terms_ref[2 * pulse, 0] + terms_ref[2 * pulse + 1, 0])
        imag_parts.append(terms_ref[2 * pulse, 1] + terms_ref[2 * pulse + 1, 1])
    real = sum(real_parts[1:], real_parts[0])
    imag = sum(imag_parts[1:], imag_parts[0])
    image_ref[0] = real
    image_ref[1] = imag
    power = real * real + imag * imag
    power_row = jnp.sum(power, axis=0, keepdims=True)
    quart_row = jnp.sum(power * power, axis=0, keepdims=True)
    for pulse in range(pulses):
        cross = imag * real_parts[pulse] - real * imag_parts[pulse]
        cross_row = jnp.sum(cross, axis=0, keepdims=True)
        power_cross_row = jnp.sum(power * cross, axis=0, keepdims=True)
        rows = jnp.concatenate((power_cross_row, cross_row, power_row, quart_row), axis=0)
        for copy in range(copies):
            sums_ref[pulse * copies + copy] = rows


def gradient_kernel(own_ref, other_ref, sums_ref, look_ref, image_ref, gradient_ref, *, pulses, npix):
    band = lax.axis_index("band")
    first = jnp.where(band == 0, own_ref[...], other_ref[...])
    second = jnp.where(band == 0, other_ref[...], own_ref[...])
    image_ref[:, :, 0:LANES] = first
    image_ref[:, :, LANES:] = second
    blocks = look_ref.shape[1] // LANES
    tiles = sums_ref.shape[0] // blocks
    weighted = jnp.zeros((4, LANES), jnp.float32)
    for block in range(blocks):
        slab, half = block // 2, block % 2
        found = sums_ref[(slab * tiles) * 2 + half]
        for tile in range(1, tiles):
            found = found + sums_ref[(slab * tiles + tile) * 2 + half]
        row = lax.broadcasted_iota(jnp.int32, (4, LANES), 0)
        look = jnp.broadcast_to(look_ref[:, block * LANES : (block + 1) * LANES], (4, LANES))
        weighted = weighted + found * jnp.where(row < 2, look, 1.0)
    totals = jnp.sum(weighted, axis=1, keepdims=True)
    mean_power = totals[2:3] / npix + power_floor
    quart = totals[3:4] / npix
    gradient = 2.0 * totals[0:1] / (mean_power * mean_power) - 2.0 * quart * totals[1:2] / (
        mean_power * mean_power * mean_power
    )
    gradient_ref[...] = jnp.broadcast_to(math.sqrt(pulses / npix) * gradient, gradient_ref.shape)


def vmem(count):
    return [pl.BlockSpec(memory_space=pltpu.VMEM)] * count


def local(echo, offsets, delta, look):
    pulses_dev, rows_dev, columns = offsets.shape
    bins = echo.shape[2]
    blocks = columns // LANES
    tiles = lax.axis_size("tile")
    pulses = lax.axis_size("pulse")
    bands = lax.axis_size("band")
    npix = rows_dev * tiles * columns
    terms = pl.pallas_call(
        terms_kernel,
        out_shape=jax.ShapeDtypeStruct((blocks, 2, rows_dev, LANES), jnp.float32),
        in_specs=[pl.BlockSpec(memory_space=pltpu.SMEM)] + vmem(3),
        out_specs=pl.BlockSpec(memory_space=pltpu.VMEM),
        scratch_shapes=[
            pltpu.VMEM((2, bins // LANES, LANES), jnp.float32),
            pltpu.VMEM((2, 1, columns), jnp.float32),
        ],
        name="terms",
    )(delta, echo, offsets, look)
    terms = lax.all_to_all(terms, ("pulse", "band"), 0, 0, tiled=True)
    half, sums = pl.pallas_call(
        image_kernel,
        out_shape=(
            jax.ShapeDtypeStruct((2, rows_dev, LANES), jnp.float32),
            jax.ShapeDtypeStruct((pulses * tiles * bands, 4, LANES), jnp.float32),
        ),
        in_specs=vmem(1),
        out_specs=vmem(2),
        name="image_sums",
    )(terms)
    other = lax.ppermute(half, "band", [(0, 1), (1, 0)])
    sums = lax.all_to_all(sums, ("pulse", "tile", "band"), 0, 0, tiled=True)
    image, gradient = pl.pallas_call(
        lambda *refs: gradient_kernel(*refs, pulses=pulses, npix=npix),
        out_shape=(
            jax.ShapeDtypeStruct((2, rows_dev, 2 * LANES), jnp.float32),
            jax.ShapeDtypeStruct((1, LANES), jnp.float32),
        ),
        in_specs=vmem(4),
        out_specs=vmem(2),
        name="gradient",
    )(half, other, sums, look)
    return image, gradient[0, 0:1]


def solution(mesh):
    in_specs = (P(None, "pulse", "band"), P("pulse", "tile", None), P("pulse"), P("pulse", None))
    out_specs = (P(None, "tile", "pulse"), P("pulse"))
    return jax.shard_map(local, mesh=mesh, in_specs=in_specs, out_specs=out_specs, check_vma=False)
```

```python
import math

import jax
import jax.numpy as jnp
from jax import lax
from jax.experimental import pallas as pl
from jax.experimental.pallas import tpu as pltpu
from jax.sharding import PartitionSpec as P

filter_taps = (-0.0136, 0.0637, -0.1804, 0.6366, 0.6366, -0.1804, 0.0637, -0.0136)
power_floor = 1e-06

LANES = 128
ROWS_DEV = 8
GROUP = 4
CHUNK = 2 * ROWS_DEV + 1
MOST = 8191.0
STEPS = 15
VMEM_BYTES = 8 * 1024 * 1024


def sine_cosine(angle):
    turns = jnp.floor(angle * (2.0 / math.pi) + 0.5)
    rest = angle - turns * 1.5703125
    rest = rest - turns * 4.837512969970703125e-4
    rest = rest - turns * 7.549789948768648e-8
    square = rest * rest
    sine = rest + rest * square * (
        -1.6666654611e-1 + square * (8.3321608736e-3 + square * -1.9515295891e-4)
    )
    cosine = 1.0 - 0.5 * square + square * square * (
        4.166664568298827e-2 + square * (-1.388731625493765e-3 + square * 2.443315711809948e-5)
    )
    quadrant = turns.astype(jnp.int32) & 3
    swap = (quadrant & 1) == 1
    sine_out = jnp.where(swap, cosine, sine)
    cosine_out = jnp.where(swap, sine, cosine)
    sine_out = jnp.where(quadrant >= 2, -sine_out, sine_out)
    cosine_out = jnp.where((quadrant == 1) | (quadrant == 2), -cosine_out, cosine_out)
    return sine_out, cosine_out


def filtered_rows(echo_rows):
    rows = echo_rows.shape[0]
    lane = lax.broadcasted_iota(jnp.int32, echo_rows.shape, 1)
    inside = filter_taps[0] * echo_rows
    across = jnp.zeros_like(echo_rows)
    for lag in range(1, 8):
        moved = filter_taps[lag] * pltpu.roll(echo_rows, LANES - lag, 1)
        here = lane < LANES - lag
        inside = inside + jnp.where(here, moved, 0.0)
        across = across + jnp.where(here, 0.0, moved)
    return inside + pltpu.roll(across, rows - 1, 0)


def lane_lookup(row, lanes):
    return jnp.take_along_axis(row, lanes, axis=1, mode="promise_in_bounds")


def table_kernel(
    delta_hbm, echo_hbm, offsets_hbm, look_hbm, table_ref, offsets_ref, look_ref, angle_ref, echo_ref, delta_ref, arrived
):
    band = lax.axis_index("band")
    slabs = offsets_ref.shape[0]
    copies = [pltpu.make_async_copy(echo_hbm, echo_ref, arrived.at[0])]
    copies.append(pltpu.make_async_copy(look_hbm, look_ref, arrived.at[1]))
    copies.append(pltpu.make_async_copy(delta_hbm, delta_ref, arrived.at[2]))
    for slab in range(slabs):
        start = pl.multiple_of((2 * slab + band) * LANES, LANES)
        copies.append(
            pltpu.make_async_copy(
                offsets_hbm.at[0, :, pl.ds(start, LANES)], offsets_ref.at[slab], arrived.at[3 + slab]
            )
        )
    for copy in copies:
        copy.start()
    lane = lax.broadcasted_iota(jnp.int32, (1, LANES), 1)
    phase_index = (lane * (5 + 2 * band)) & 63
    sine, cosine = sine_cosine(phase_index.astype(jnp.float32) * (math.pi / 32.0))
    copies[0].wait()
    filt = []
    for part in range(2):
        rows = echo_ref[part : part + 1].astype(jnp.float32).reshape(table_ref.shape[1], LANES)
        filt.append(filtered_rows(rows))
    table_ref[0] = cosine * filt[0] - sine * filt[1]
    table_ref[1] = sine * filt[0] + cosine * filt[1]
    copies[1].wait()
    copies[2].wait()
    angle_ref[...] = delta_ref[...] * look_ref[...]
    for copy in copies[3:]:
        copy.wait()


def pack(table_ref, words_ref):
    real, imag = table_ref[0], table_ref[1]
    size = jnp.maximum(jnp.abs(real), jnp.abs(imag))
    top = jnp.max(jnp.max(size, axis=0, keepdims=True), axis=1, keepdims=True)
    top = jnp.where(top > 0.0, top, 1.0)
    shrink = 1.0 / top
    size = size * shrink
    power = jnp.zeros(size.shape, jnp.int32)
    for step in range(1, STEPS + 1):
        power = power + jnp.where(size > 2.0**-step, 1, 0)
    grow = (1 << (STEPS - power)).astype(jnp.float32) * MOST
    real = jnp.floor(real * shrink * grow + 0.5).astype(jnp.int32)
    imag = jnp.floor(imag * shrink * grow + 0.5).astype(jnp.int32)
    words_ref[...] = (real << 18) | ((imag & 0x3FFF) << 4) | power
    return top


def unpack(word):
    unit = (1 << (word & 15)).astype(jnp.float32) * (1.0 / (MOST * 2.0**STEPS))
    return (word >> 18).astype(jnp.float32) * unit, ((word << 14) >> 18).astype(jnp.float32) * unit


def look_up(words_ref, offsets):
    lanes = offsets & (LANES - 1)
    high = offsets >> 7
    found = None
    for row in range(words_ref.shape[0]):
        spread = jnp.broadcast_to(words_ref[pl.ds(row, 1), :], offsets.shape)
        here = lane_lookup(spread, lanes)
        found = here if row == 0 else jnp.where(high == row, here, found)
    return found


def own_kernel(table_ref, offsets_ref, angle_ref, out_ref, turn_ref, words_ref):
    slabs = out_ref.shape[0]
    band = lax.axis_index("band")
    top = pack(table_ref, words_ref)

    def some_blocks(step, carry):
        for j in range(GROUP):
            slab = step * GROUP + j
            real, imag = unpack(look_up(words_ref, offsets_ref[slab]))
            out_ref[slab, 0] = top * real
            out_ref[slab, 1] = top * imag
            start = pl.multiple_of((2 * slab + band) * LANES, LANES)
            sine, cosine = sine_cosine(angle_ref[:, pl.ds(start, LANES)])
            turn_ref[slab, 0:1] = cosine
            turn_ref[slab, 1:2] = sine
        return carry

    lax.fori_loop(0, slabs // GROUP, some_blocks, 0)


def other_kernel(table_ref, offsets_ref, look_ref, own_ref, turn_ref, out_ref, words_ref):
    slabs = own_ref.shape[0]
    band = lax.axis_index("band")
    top = pack(table_ref, words_ref)

    def some_blocks(step, carry):
        for j in range(GROUP):
            slab = step * GROUP + j
            real, imag = unpack(look_up(words_ref, offsets_ref[slab]))
            real = own_ref[slab, 0] + top * real
            imag = own_ref[slab, 1] + top * imag
            cosine = turn_ref[slab, 0:1]
            sine = turn_ref[slab, 1:2]
            first = slab * CHUNK
            out_ref[pl.ds(first, ROWS_DEV), 0, :] = cosine * real - sine * imag
            out_ref[pl.ds(first + ROWS_DEV, ROWS_DEV), 0, :] = sine * real + cosine * imag
            start = pl.multiple_of((2 * slab + band) * LANES, LANES)
            out_ref[first + 2 * ROWS_DEV] = look_ref[:, pl.ds(start, LANES)]
        return carry

    lax.fori_loop(0, slabs // GROUP, some_blocks, 0)


def image_kernel(terms_ref, image_ref, sums_ref):
    pulses = terms_ref.shape[0] // CHUNK
    copies = sums_ref.shape[0] // pulses
    reals = [terms_ref[p * CHUNK : p * CHUNK + ROWS_DEV, 0, :] for p in range(pulses)]
    imags = [terms_ref[p * CHUNK + ROWS_DEV : p * CHUNK + 2 * ROWS_DEV, 0, :] for p in range(pulses)]
    looks = [terms_ref[p * CHUNK + 2 * ROWS_DEV] for p in range(pulses)]
    real = sum(reals[1:], reals[0])
    imag = sum(imags[1:], imags[0])
    image_ref[0] = real
    image_ref[1] = imag
    power = real * real + imag * imag
    power_sum = jnp.sum(jnp.sum(power, axis=0, keepdims=True), axis=1, keepdims=True)
    quart_sum = jnp.sum(jnp.sum(power * power, axis=0, keepdims=True), axis=1, keepdims=True)
    cross_rows, power_cross_rows = [], []
    for p in range(pulses):
        cross = imag * reals[p] - real * imags[p]
        cross_rows.append(looks[p] * jnp.sum(cross, axis=0, keepdims=True))
        power_cross_rows.append(looks[p] * jnp.sum(power * cross, axis=0, keepdims=True))
    cross_sums = jnp.sum(jnp.concatenate(cross_rows, axis=0), axis=1, keepdims=True)
    power_cross_sums = jnp.sum(jnp.concatenate(power_cross_rows, axis=0), axis=1, keepdims=True)
    lane = lax.broadcasted_iota(jnp.int32, (pulses, LANES), 1)
    sums = jnp.where(lane == 0, power_cross_sums, 0.0) + jnp.where(lane == 1, cross_sums, 0.0)
    sums = sums + jnp.where(lane == 2, power_sum, 0.0) + jnp.where(lane == 3, quart_sum, 0.0)
    for p in range(pulses):
        sums_ref[p * copies : (p + 1) * copies, 0, :] = jnp.broadcast_to(sums[p : p + 1], (copies, LANES))


def join_kernel(own_ref, other_ref, image_ref):
    band = lax.axis_index("band")
    image_ref[:, :, 0:LANES] = jnp.where(band == 0, own_ref[...], other_ref[...])
    image_ref[:, :, LANES:] = jnp.where(band == 0, other_ref[...], own_ref[...])


def gradient_kernel(sums_ref, gradient_ref, *, pulses, npix):
    totals = jnp.sum(sums_ref[:, 0, :], axis=0, keepdims=True)
    mean_power = totals[:, 2:3] / npix + power_floor
    quart = totals[:, 3:4] / npix
    gradient = 2.0 * totals[:, 0:1] / (mean_power * mean_power) - 2.0 * quart * totals[:, 1:2] / (
        mean_power * mean_power * mean_power
    )
    gradient_ref[...] = jnp.broadcast_to(math.sqrt(pulses / npix) * gradient, gradient_ref.shape)


SMEM, VMEM, HBM = (pl.BlockSpec(memory_space=space) for space in (pltpu.SMEM, pltpu.VMEM, pltpu.HBM))


def on_device(kernel, out, *operands, name, spaces=None, scratch=(), flops=0):
    return pl.pallas_call(
        kernel,
        out_shape=tuple(jax.ShapeDtypeStruct(shape, dtype) for shape, dtype in out),
        in_specs=spaces or [VMEM] * len(operands),
        out_specs=(VMEM,) * len(out),
        scratch_shapes=scratch,
        compiler_params=pltpu.CompilerParams(vmem_limit_bytes=VMEM_BYTES),
        cost_estimate=pl.CostEstimate(flops=flops, bytes_accessed=1 << 20, transcendentals=0),
        name=name,
    )(*operands)


def local(echo, offsets, delta, look):
    rows_dev, columns = offsets.shape[1:]
    bins = echo.shape[2]
    tiles = lax.axis_size("tile")
    pulses = lax.axis_size("pulse")
    bands = lax.axis_size("band")
    slabs = columns // (LANES * bands)
    npix = rows_dev * tiles * columns
    swap = [(0, 1), (1, 0)]
    f32, i32 = jnp.float32, jnp.int32
    table_shape = (2, bins // LANES, LANES)
    words = pltpu.VMEM(table_shape[1:], i32)
    half_shape = (2, rows_dev, LANES)

    inputs = (delta.reshape(1, 1), echo.reshape(2, bins), offsets, look)
    table, own_offsets, look, angle = on_device(
        table_kernel,
        [(table_shape, f32), ((slabs, rows_dev, LANES), i32), ((1, columns), f32), ((1, columns), f32)],
        inputs[0], *(pltpu.with_memory_space_constraint(array, pltpu.HBM) for array in inputs[1:]),
        name="table", spaces=[pl.BlockSpec(memory_space=pl.ANY)] + [HBM] * 3,
        scratch=[
            pltpu.VMEM((2, bins), echo.dtype),
            pltpu.VMEM((1, 1), f32),
            pltpu.SemaphoreType.DMA((3 + slabs,)),
        ],
    )
    other_table = lax.ppermute(table, "band", swap)
    own, turn = on_device(
        own_kernel,
        [((slabs,) + half_shape, f32), ((slabs, 2, LANES), f32)],
        table, own_offsets, angle,
        name="own_lookup", scratch=[words], flops=1 << 30,
    )
    (terms,) = on_device(
        other_kernel,
        [((slabs * CHUNK, 1, LANES), f32)],
        other_table, own_offsets, look, own, turn,
        name="other_lookup", scratch=[words],
    )
    terms = lax.all_to_all(terms, "pulse", 0, 0, tiled=True)
    half, sums = on_device(
        image_kernel, [(half_shape, f32), ((pulses * tiles * bands, 1, LANES), f32)], terms, name="image_sums"
    )
    other_half = lax.ppermute(half, "band", swap)
    sums = lax.all_to_all(sums, ("pulse", "tile", "band"), 0, 0, tiled=True)
    (image,) = on_device(join_kernel, [((2, rows_dev, 2 * LANES), f32)], half, other_half, name="join")
    (gradient,) = on_device(
        lambda *refs: gradient_kernel(*refs, pulses=pulses, npix=npix), [((1, LANES), f32)], sums, name="gradient"
    )
    return image, gradient[0, 0:1]


def solution(mesh):
    in_specs = (P(None, "pulse", "band"), P("pulse", "tile", None), P("pulse"), P("pulse", None))
    out_specs = (P(None, "tile", "pulse"), P("pulse"))
    return jax.shard_map(local, mesh=mesh, in_specs=in_specs, out_specs=out_specs, check_vma=False)
```

```python
import math

import jax
import jax.numpy as jnp
from jax import lax
from jax.experimental import pallas as pl
from jax.experimental.pallas import tpu as pltpu
from jax.sharding import PartitionSpec as P

filter_taps = (-0.0136, 0.0637, -0.1804, 0.6366, 0.6366, -0.1804, 0.0637, -0.0136)
power_floor = 1e-06

LANES = 128
ROWS_DEV = 8
GROUP = 16
CHUNK = 2 * ROWS_DEV + 1
MOST = 32767.0
VMEM_BYTES = 8 * 1024 * 1024


def sine_cosine(angle):
    turns = jnp.floor(angle * (2.0 / math.pi) + 0.5)
    rest = angle - turns * 1.5703125
    rest = rest - turns * 4.837512969970703125e-4
    rest = rest - turns * 7.549789948768648e-8
    square = rest * rest
    sine = rest + rest * square * (
        -1.6666654611e-1 + square * (8.3321608736e-3 + square * -1.9515295891e-4)
    )
    cosine = 1.0 - 0.5 * square + square * square * (
        4.166664568298827e-2 + square * (-1.388731625493765e-3 + square * 2.443315711809948e-5)
    )
    quadrant = turns.astype(jnp.int32) & 3
    swap = (quadrant & 1) == 1
    sine_out = jnp.where(swap, cosine, sine)
    cosine_out = jnp.where(swap, sine, cosine)
    sine_out = jnp.where(quadrant >= 2, -sine_out, sine_out)
    cosine_out = jnp.where((quadrant == 1) | (quadrant == 2), -cosine_out, cosine_out)
    return sine_out, cosine_out


def filtered_rows(echo_rows):
    rows = echo_rows.shape[0]
    lane = lax.broadcasted_iota(jnp.int32, echo_rows.shape, 1)
    inside = filter_taps[0] * echo_rows
    across = jnp.zeros_like(echo_rows)
    for lag in range(1, 8):
        moved = filter_taps[lag] * pltpu.roll(echo_rows, LANES - lag, 1)
        here = lane < LANES - lag
        inside = inside + jnp.where(here, moved, 0.0)
        across = across + jnp.where(here, 0.0, moved)
    return inside + pltpu.roll(across, rows - 1, 0)


def lane_lookup(row, lanes):
    return jnp.take_along_axis(row, lanes, axis=1, mode="promise_in_bounds")


def table_kernel(
    delta_hbm, echo_hbm, offsets_hbm, look_hbm, table_ref, offsets_ref, look_ref, angle_ref, echo_ref, delta_ref, arrived
):
    band = lax.axis_index("band")
    slabs = offsets_ref.shape[0]
    copies = [pltpu.make_async_copy(echo_hbm, echo_ref, arrived.at[0])]
    copies.append(pltpu.make_async_copy(look_hbm, look_ref, arrived.at[1]))
    copies.append(pltpu.make_async_copy(delta_hbm, delta_ref, arrived.at[2]))
    for slab in range(slabs):
        start = pl.multiple_of((2 * slab + band) * LANES, LANES)
        copies.append(
            pltpu.make_async_copy(
                offsets_hbm.at[0, :, pl.ds(start, LANES)], offsets_ref.at[slab], arrived.at[3 + slab]
            )
        )
    for copy in copies:
        copy.start()
    lane = lax.broadcasted_iota(jnp.int32, (1, LANES), 1)
    phase_index = (lane * (5 + 2 * band)) & 63
    sine, cosine = sine_cosine(phase_index.astype(jnp.float32) * (math.pi / 32.0))
    copies[0].wait()
    filt = []
    for part in range(2):
        rows = echo_ref[part : part + 1].astype(jnp.float32).reshape(table_ref.shape[1], LANES)
        filt.append(filtered_rows(rows))
    table_ref[0] = cosine * filt[0] - sine * filt[1]
    table_ref[1] = sine * filt[0] + cosine * filt[1]
    copies[1].wait()
    copies[2].wait()
    angle_ref[...] = delta_ref[...] * look_ref[...]
    for copy in copies[3:]:
        copy.wait()


def pack(table_ref, words_ref):
    real, imag = table_ref[0], table_ref[1]
    rows = real.shape[0]
    size = jnp.maximum(jnp.abs(real), jnp.abs(imag))
    lane = lax.broadcasted_iota(jnp.int32, size.shape, 1)
    row = lax.broadcasted_iota(jnp.int32, size.shape, 0)
    first_half = lane < LANES // 2
    tops = []
    for half in range(2):
        inside = first_half if half == 0 else jnp.logical_not(first_half)
        top = jnp.max(jnp.where(inside, size, 0.0), axis=1, keepdims=True)
        tops.append(jnp.where(top > 0.0, top, 1.0))
    shrink = jnp.where(first_half, 1.0 / tops[0], 1.0 / tops[1])
    real = jnp.floor(real * shrink * MOST + 0.5).astype(jnp.int32)
    imag = jnp.floor(imag * shrink * MOST + 0.5).astype(jnp.int32)
    words_ref[...] = (real << 16) | (imag & 0xFFFF)
    spread = jnp.where(lane == row, tops[0], 0.0) + jnp.where(lane == row + rows, tops[1], 0.0)
    return jnp.sum(spread, axis=0, keepdims=True)


def look_up(words_ref, tops, offsets):
    rows = words_ref.shape[0]
    lanes = offsets & (LANES - 1)
    high = offsets >> 7
    top = lane_lookup(jnp.broadcast_to(tops, offsets.shape), high + ((offsets & 64) * (rows // 64)))
    found = None
    for row in range(rows):
        spread = jnp.broadcast_to(words_ref[pl.ds(row, 1), :], offsets.shape)
        here = lane_lookup(spread, lanes)
        found = here if row == 0 else jnp.where(high == row, here, found)
    real = (found >> 16).astype(jnp.float32)
    imag = ((found << 16) >> 16).astype(jnp.float32)
    return real * (1.0 / MOST) * top, imag * (1.0 / MOST) * top


def own_kernel(table_ref, offsets_ref, angle_ref, out_ref, turn_ref, words_ref):
    slabs = out_ref.shape[0]
    band = lax.axis_index("band")
    tops = pack(table_ref, words_ref)

    def some_blocks(step, carry):
        for j in range(GROUP):
            slab = step * GROUP + j
            real, imag = look_up(words_ref, tops, offsets_ref[slab])
            out_ref[slab, 0] = real
            out_ref[slab, 1] = imag
            start = pl.multiple_of((2 * slab + band) * LANES, LANES)
            sine, cosine = sine_cosine(angle_ref[:, pl.ds(start, LANES)])
            turn_ref[slab, 0:1] = cosine
            turn_ref[slab, 1:2] = sine
        return carry

    lax.fori_loop(0, slabs // GROUP, some_blocks, 0)


def other_kernel(table_ref, offsets_ref, look_ref, own_ref, turn_ref, out_ref, words_ref):
    slabs = own_ref.shape[0]
    band = lax.axis_index("band")
    tops = pack(table_ref, words_ref)

    def some_blocks(step, carry):
        for j in range(GROUP):
            slab = step * GROUP + j
            real, imag = look_up(words_ref, tops, offsets_ref[slab])
            real = own_ref[slab, 0] + real
            imag = own_ref[slab, 1] + imag
            cosine = turn_ref[slab, 0:1]
            sine = turn_ref[slab, 1:2]
            first = slab * CHUNK
            out_ref[pl.ds(first, ROWS_DEV), 0, :] = cosine * real - sine * imag
            out_ref[pl.ds(first + ROWS_DEV, ROWS_DEV), 0, :] = sine * real + cosine * imag
            start = pl.multiple_of((2 * slab + band) * LANES, LANES)
            out_ref[first + 2 * ROWS_DEV] = look_ref[:, pl.ds(start, LANES)]
        return carry

    lax.fori_loop(0, slabs // GROUP, some_blocks, 0)


def image_kernel(terms_ref, image_ref, sums_ref):
    pulses = terms_ref.shape[0] // CHUNK
    copies = sums_ref.shape[0] // pulses
    reals = [terms_ref[p * CHUNK : p * CHUNK + ROWS_DEV, 0, :] for p in range(pulses)]
    imags = [terms_ref[p * CHUNK + ROWS_DEV : p * CHUNK + 2 * ROWS_DEV, 0, :] for p in range(pulses)]
    looks = [terms_ref[p * CHUNK + 2 * ROWS_DEV] for p in range(pulses)]
    real = sum(reals[1:], reals[0])
    imag = sum(imags[1:], imags[0])
    image_ref[0] = real
    image_ref[1] = imag
    power = real * real + imag * imag
    power_sum = jnp.sum(jnp.sum(power, axis=0, keepdims=True), axis=1, keepdims=True)
    quart_sum = jnp.sum(jnp.sum(power * power, axis=0, keepdims=True), axis=1, keepdims=True)
    cross_rows, power_cross_rows = [], []
    for p in range(pulses):
        cross = imag * reals[p] - real * imags[p]
        cross_rows.append(looks[p] * jnp.sum(cross, axis=0, keepdims=True))
        power_cross_rows.append(looks[p] * jnp.sum(power * cross, axis=0, keepdims=True))
    cross_sums = jnp.sum(jnp.concatenate(cross_rows, axis=0), axis=1, keepdims=True)
    power_cross_sums = jnp.sum(jnp.concatenate(power_cross_rows, axis=0), axis=1, keepdims=True)
    lane = lax.broadcasted_iota(jnp.int32, (pulses, LANES), 1)
    sums = jnp.where(lane == 0, power_cross_sums, 0.0) + jnp.where(lane == 1, cross_sums, 0.0)
    sums = sums + jnp.where(lane == 2, power_sum, 0.0) + jnp.where(lane == 3, quart_sum, 0.0)
    for p in range(pulses):
        sums_ref[p * copies : (p + 1) * copies, 0, :] = jnp.broadcast_to(sums[p : p + 1], (copies, LANES))


def join_kernel(own_ref, other_ref, image_ref):
    band = lax.axis_index("band")
    image_ref[:, :, 0:LANES] = jnp.where(band == 0, own_ref[...], other_ref[...])
    image_ref[:, :, LANES:] = jnp.where(band == 0, other_ref[...], own_ref[...])


def gradient_kernel(sums_ref, gradient_ref, *, pulses, npix):
    totals = jnp.sum(sums_ref[:, 0, :], axis=0, keepdims=True)
    mean_power = totals[:, 2:3] / npix + power_floor
    quart = totals[:, 3:4] / npix
    gradient = 2.0 * totals[:, 0:1] / (mean_power * mean_power) - 2.0 * quart * totals[:, 1:2] / (
        mean_power * mean_power * mean_power
    )
    gradient_ref[...] = jnp.broadcast_to(math.sqrt(pulses / npix) * gradient, gradient_ref.shape)


SMEM, VMEM, HBM = (pl.BlockSpec(memory_space=space) for space in (pltpu.SMEM, pltpu.VMEM, pltpu.HBM))


def on_device(kernel, out, *operands, name, spaces=None, scratch=(), flops=0):
    return pl.pallas_call(
        kernel,
        out_shape=tuple(jax.ShapeDtypeStruct(shape, dtype) for shape, dtype in out),
        in_specs=spaces or [VMEM] * len(operands),
        out_specs=(VMEM,) * len(out),
        scratch_shapes=scratch,
        compiler_params=pltpu.CompilerParams(vmem_limit_bytes=VMEM_BYTES),
        cost_estimate=pl.CostEstimate(flops=flops, bytes_accessed=1 << 20, transcendentals=0),
        name=name,
    )(*operands)


def local(echo, offsets, delta, look):
    rows_dev, columns = offsets.shape[1:]
    bins = echo.shape[2]
    tiles = lax.axis_size("tile")
    pulses = lax.axis_size("pulse")
    bands = lax.axis_size("band")
    slabs = columns // (LANES * bands)
    npix = rows_dev * tiles * columns
    swap = [(0, 1), (1, 0)]
    f32, i32 = jnp.float32, jnp.int32
    table_shape = (2, bins // LANES, LANES)
    words = pltpu.VMEM(table_shape[1:], i32)
    half_shape = (2, rows_dev, LANES)

    inputs = (delta.reshape(1, 1), echo.reshape(2, bins), offsets, look)
    table, own_offsets, look, angle = on_device(
        table_kernel,
        [(table_shape, f32), ((slabs, rows_dev, LANES), i32), ((1, columns), f32), ((1, columns), f32)],
        inputs[0], *(pltpu.with_memory_space_constraint(array, pltpu.HBM) for array in inputs[1:]),
        name="table", spaces=[pl.BlockSpec(memory_space=pl.ANY)] + [HBM] * 3,
        scratch=[
            pltpu.VMEM((2, bins), echo.dtype),
            pltpu.VMEM((1, 1), f32),
            pltpu.SemaphoreType.DMA((3 + slabs,)),
        ],
    )
    other_table = lax.ppermute(table, "band", swap)
    own, turn = on_device(
        own_kernel,
        [((slabs,) + half_shape, f32), ((slabs, 2, LANES), f32)],
        table, own_offsets, angle,
        name="own_lookup", scratch=[words], flops=1 << 30,
    )
    (terms,) = on_device(
        other_kernel,
        [((slabs * CHUNK, 1, LANES), f32)],
        other_table, own_offsets, look, own, turn,
        name="other_lookup", scratch=[words],
    )
    terms = lax.all_to_all(terms, "pulse", 0, 0, tiled=True)
    half, sums = on_device(
        image_kernel, [(half_shape, f32), ((pulses * tiles * bands, 1, LANES), f32)], terms, name="image_sums"
    )
    other_half = lax.ppermute(half, "band", swap)
    sums = lax.all_to_all(sums, ("pulse", "tile", "band"), 0, 0, tiled=True)
    (image,) = on_device(join_kernel, [((2, rows_dev, 2 * LANES), f32)], half, other_half, name="join")
    (gradient,) = on_device(
        lambda *refs: gradient_kernel(*refs, pulses=pulses, npix=npix), [((1, LANES), f32)], sums, name="gradient"
    )
    return image, gradient[0, 0:1]


def solution(mesh):
    in_specs = (P(None, "pulse", "band"), P("pulse", "tile", None), P("pulse"), P("pulse", None))
    out_specs = (P(None, "tile", "pulse"), P("pulse"))
    return jax.shard_map(local, mesh=mesh, in_specs=in_specs, out_specs=out_specs, check_vma=False)
```

```python
import math

import jax
import jax.numpy as jnp
from jax import lax
from jax.experimental import pallas as pl
from jax.experimental.pallas import tpu as pltpu
from jax.sharding import PartitionSpec as P

filter_taps = (-0.0136, 0.0637, -0.1804, 0.6366, 0.6366, -0.1804, 0.0637, -0.0136)
power_floor = 1e-06

LANES = 128
ROWS_DEV = 8
CHUNK = 2 * ROWS_DEV + 1
MOST = 32767.0
CHAIN = 16
VMEM_BYTES = 8 * 1024 * 1024


def sine_cosine(angle):
    turns = jnp.floor(angle * (2.0 / math.pi) + 0.5)
    rest = angle - turns * 1.5703125
    rest = rest - turns * 4.837512969970703125e-4
    rest = rest - turns * 7.549789948768648e-8
    square = rest * rest
    sine = rest + rest * square * (
        -1.6666654611e-1 + square * (8.3321608736e-3 + square * -1.9515295891e-4)
    )
    cosine = 1.0 - 0.5 * square + square * square * (
        4.166664568298827e-2 + square * (-1.388731625493765e-3 + square * 2.443315711809948e-5)
    )
    quadrant = turns.astype(jnp.int32) & 3
    swap = (quadrant & 1) == 1
    sine_out = jnp.where(swap, cosine, sine)
    cosine_out = jnp.where(swap, sine, cosine)
    sine_out = jnp.where(quadrant >= 2, -sine_out, sine_out)
    cosine_out = jnp.where((quadrant == 1) | (quadrant == 2), -cosine_out, cosine_out)
    return sine_out, cosine_out


def filtered_rows(echo_rows):
    rows = echo_rows.shape[0]
    lane = lax.broadcasted_iota(jnp.int32, echo_rows.shape, 1)
    inside = filter_taps[0] * echo_rows
    across = jnp.zeros_like(echo_rows)
    for lag in range(1, 8):
        moved = filter_taps[lag] * pltpu.roll(echo_rows, LANES - lag, 1)
        here = lane < LANES - lag
        inside = inside + jnp.where(here, moved, 0.0)
        across = across + jnp.where(here, 0.0, moved)
    return inside + pltpu.roll(across, rows - 1, 0)


def lane_lookup(row, lanes):
    return jnp.take_along_axis(row, lanes, axis=1, mode="promise_in_bounds")


def table_kernel(echo_hbm, offsets_hbm, look_hbm, table_ref, offsets_ref, look_ref, echo_ref, arrived):
    band = lax.axis_index("band")
    copies = [
        pltpu.make_async_copy(echo_hbm, echo_ref, arrived.at[0]),
        pltpu.make_async_copy(look_hbm, look_ref, arrived.at[1]),
    ]
    for slab in range(offsets_ref.shape[0]):
        block = pl.ds(pl.multiple_of((2 * slab + band) * LANES, LANES), LANES)
        copies.append(
            pltpu.make_async_copy(offsets_hbm.at[0, :, block], offsets_ref.at[slab], arrived.at[2 + slab])
        )
    for copy in copies:
        copy.start()
    lane = lax.broadcasted_iota(jnp.int32, (1, LANES), 1)
    phase_index = (lane * (5 + 2 * band)) & 63
    sine, cosine = sine_cosine(phase_index.astype(jnp.float32) * (math.pi / 32.0))
    copies[0].wait()
    filt = []
    for part in range(2):
        rows = echo_ref[part : part + 1].astype(jnp.float32).reshape(table_ref.shape[1], LANES)
        filt.append(filtered_rows(rows))
    table_ref[0] = cosine * filt[0] - sine * filt[1]
    table_ref[1] = sine * filt[0] + cosine * filt[1]
    for copy in copies[1:]:
        copy.wait()


def turn_kernel(delta_ref, look_ref, own_look_ref, turn_ref):
    band = lax.axis_index("band")
    for slab in range(own_look_ref.shape[0]):
        block = pl.ds(pl.multiple_of((2 * slab + band) * LANES, LANES), LANES)
        own_look_ref[slab : slab + 1] = look_ref[:, block]
    sine, cosine = sine_cosine(delta_ref[0] * own_look_ref[...])
    turn_ref[0] = cosine
    turn_ref[1] = sine


def pack(real, imag, words_ref):
    rows = real.shape[0]
    size = jnp.maximum(jnp.abs(real), jnp.abs(imag))
    lane = lax.broadcasted_iota(jnp.int32, size.shape, 1)
    row = lax.broadcasted_iota(jnp.int32, size.shape, 0)
    first_half = lane < LANES // 2
    tops = []
    for half in range(2):
        inside = first_half if half == 0 else jnp.logical_not(first_half)
        top = jnp.max(jnp.where(inside, size, 0.0), axis=1, keepdims=True)
        tops.append(jnp.where(top > 0.0, top, 1.0))
    shrink = jnp.where(first_half, 1.0 / tops[0], 1.0 / tops[1])
    real = jnp.floor(real * shrink * MOST + 0.5).astype(jnp.int32)
    imag = jnp.floor(imag * shrink * MOST + 0.5).astype(jnp.int32)
    words_ref[...] = (real << 16) | (imag & 0xFFFF)
    spread = jnp.where(lane == row, tops[0], 0.0) + jnp.where(lane == row + rows, tops[1], 0.0)
    return jnp.sum(spread, axis=0, keepdims=True)


def look_up(words_ref, tops, offsets):
    rows = words_ref.shape[0]
    lanes = offsets & (LANES - 1)
    high = offsets >> 7
    top = lane_lookup(jnp.broadcast_to(tops, offsets.shape), high + ((offsets & 64) * (rows // 64)))
    low = high & (CHAIN - 1)
    chains = [None] * (rows // CHAIN)
    for step in range(CHAIN):
        match = low == step
        for chain in range(len(chains)):
            row = chain * CHAIN + step
            here = lane_lookup(jnp.broadcast_to(words_ref[pl.ds(row, 1), :], offsets.shape), lanes)
            chains[chain] = here if step == 0 else jnp.where(match, here, chains[chain])
    found = chains[0]
    for chain in range(1, len(chains)):
        found = jnp.where(high >= chain * CHAIN, chains[chain], found)
    real = (found >> 16).astype(jnp.float32)
    imag = ((found << 16) >> 16).astype(jnp.float32)
    return real * (1.0 / MOST) * top, imag * (1.0 / MOST) * top


def terms_kernel(own_ref, other_ref, offsets_ref, look_ref, turn_ref, out_ref, words_ref):
    tops = pack(own_ref[0] + other_ref[0], own_ref[1] + other_ref[1], words_ref)
    for slab in range(offsets_ref.shape[0]):
        real, imag = look_up(words_ref, tops, offsets_ref[slab])
        cosine = turn_ref[0, slab : slab + 1]
        sine = turn_ref[1, slab : slab + 1]
        first = slab * CHUNK
        out_ref[first : first + ROWS_DEV, 0, :] = cosine * real - sine * imag
        out_ref[first + ROWS_DEV : first + 2 * ROWS_DEV, 0, :] = sine * real + cosine * imag
        out_ref[first + 2 * ROWS_DEV] = look_ref[slab : slab + 1]


def image_kernel(terms_ref, image_ref, sums_ref):
    pulses = terms_ref.shape[0] // CHUNK
    copies = sums_ref.shape[0] // pulses
    reals = [terms_ref[p * CHUNK : p * CHUNK + ROWS_DEV, 0, :] for p in range(pulses)]
    imags = [terms_ref[p * CHUNK + ROWS_DEV : p * CHUNK + 2 * ROWS_DEV, 0, :] for p in range(pulses)]
    looks = [terms_ref[p * CHUNK + 2 * ROWS_DEV] for p in range(pulses)]
    real = sum(reals[1:], reals[0])
    imag = sum(imags[1:], imags[0])
    image_ref[0] = real
    image_ref[1] = imag
    power = real * real + imag * imag
    power_sum = jnp.sum(jnp.sum(power, axis=0, keepdims=True), axis=1, keepdims=True)
    quart_sum = jnp.sum(jnp.sum(power * power, axis=0, keepdims=True), axis=1, keepdims=True)
    cross_rows, power_cross_rows = [], []
    for p in range(pulses):
        cross = imag * reals[p] - real * imags[p]
        cross_rows.append(looks[p] * jnp.sum(cross, axis=0, keepdims=True))
        power_cross_rows.append(looks[p] * jnp.sum(power * cross, axis=0, keepdims=True))
    cross_sums = jnp.sum(jnp.concatenate(cross_rows, axis=0), axis=1, keepdims=True)
    power_cross_sums = jnp.sum(jnp.concatenate(power_cross_rows, axis=0), axis=1, keepdims=True)
    lane = lax.broadcasted_iota(jnp.int32, (pulses, LANES), 1)
    sums = jnp.where(lane == 0, power_cross_sums, 0.0) + jnp.where(lane == 1, cross_sums, 0.0)
    sums = sums + jnp.where(lane == 2, power_sum, 0.0) + jnp.where(lane == 3, quart_sum, 0.0)
    for copy in range(copies):
        sums_ref[copy * pulses : (copy + 1) * pulses, 0, :] = sums


def join_kernel(own_ref, other_ref, image_ref):
    band = lax.axis_index("band")
    image_ref[:, :, 0:LANES] = jnp.where(band == 0, own_ref[...], other_ref[...])
    image_ref[:, :, LANES:] = jnp.where(band == 0, other_ref[...], own_ref[...])


def gradient_kernel(sums_ref, gradient_ref, *, pulses, npix):
    totals = jnp.sum(sums_ref[:, 0, :], axis=0, keepdims=True)
    mean_power = totals[:, 2:3] / npix + power_floor
    quart = totals[:, 3:4] / npix
    gradient = 2.0 * totals[:, 0:1] / (mean_power * mean_power) - 2.0 * quart * totals[:, 1:2] / (
        mean_power * mean_power * mean_power
    )
    gradient_ref[...] = jnp.broadcast_to(math.sqrt(pulses / npix) * gradient, gradient_ref.shape)


SMEM, VMEM, HBM = (pl.BlockSpec(memory_space=space) for space in (pltpu.SMEM, pltpu.VMEM, pltpu.HBM))


def on_device(kernel, out, *operands, name, spaces=None, scratch=(), flops=0):
    return pl.pallas_call(
        kernel,
        out_shape=tuple(jax.ShapeDtypeStruct(shape, dtype) for shape, dtype in out),
        in_specs=spaces or [VMEM] * len(operands),
        out_specs=(VMEM,) * len(out),
        scratch_shapes=scratch,
        compiler_params=pltpu.CompilerParams(vmem_limit_bytes=VMEM_BYTES),
        cost_estimate=pl.CostEstimate(flops=flops, bytes_accessed=1 << 20, transcendentals=0),
        name=name,
    )(*operands)


def local(echo, offsets, delta, look):
    rows_dev, columns = offsets.shape[1:]
    bins = echo.shape[2]
    tiles = lax.axis_size("tile")
    pulses = lax.axis_size("pulse")
    bands = lax.axis_size("band")
    slabs = columns // (LANES * bands)
    npix = rows_dev * tiles * columns
    swap = [(0, 1), (1, 0)]
    f32, i32 = jnp.float32, jnp.int32
    table_shape = (2, bins // LANES, LANES)
    half_shape = (2, rows_dev, LANES)
    columns_shape = (slabs, LANES)

    inputs = (echo.reshape(2, bins), offsets, look)
    table, own_offsets, look = on_device(
        table_kernel,
        [(table_shape, f32), ((slabs, rows_dev, LANES), i32), ((1, columns), f32)],
        *(pltpu.with_memory_space_constraint(array, pltpu.HBM) for array in inputs),
        name="table", spaces=[HBM] * 3,
        scratch=[pltpu.VMEM((2, bins), echo.dtype), pltpu.SemaphoreType.DMA((2 + slabs,))],
    )
    other_table = lax.ppermute(table, "band", swap)
    own_look, turn = on_device(
        turn_kernel,
        [(columns_shape, f32), ((2,) + columns_shape, f32)],
        delta, look,
        name="turn", spaces=[SMEM, VMEM], flops=1 << 30,
    )
    (terms,) = on_device(
        terms_kernel,
        [((slabs * CHUNK, 1, LANES), f32)],
        table, other_table, own_offsets, own_look, turn,
        name="terms", scratch=[pltpu.VMEM(table_shape[1:], i32)],
    )
    terms = lax.all_to_all(terms, "pulse", 0, 0, tiled=True)
    half, sums = on_device(
        image_kernel, [(half_shape, f32), ((pulses * tiles * bands, 1, LANES), f32)], terms, name="image_sums"
    )
    other_half = lax.ppermute(half, "band", swap)
    sums = lax.all_to_all(sums, ("band", "tile", "pulse"), 0, 0, tiled=True)
    (image,) = on_device(join_kernel, [((2, rows_dev, 2 * LANES), f32)], half, other_half, name="join")
    (gradient,) = on_device(
        lambda *refs: gradient_kernel(*refs, pulses=pulses, npix=npix), [((1, LANES), f32)], sums, name="gradient"
    )
    return image, gradient[0, 0:1]


def solution(mesh):
    in_specs = (P(None, "pulse", "band"), P("pulse", "tile", None), P("pulse"), P("pulse", None))
    out_specs = (P(None, "tile", "pulse"), P("pulse"))
    return jax.shard_map(local, mesh=mesh, in_specs=in_specs, out_specs=out_specs, check_vma=False)
```

```python
import math

import jax
import jax.numpy as jnp
from jax import lax
from jax.experimental import pallas as pl
from jax.experimental.pallas import tpu as pltpu
from jax.sharding import PartitionSpec as P

filter_taps = (-0.0136, 0.0637, -0.1804, 0.6366, 0.6366, -0.1804, 0.0637, -0.0136)
power_floor = 1e-06

LANES = 128
ROWS_DEV = 8
CHUNK = 2 * ROWS_DEV + 1
MOST = 32767.0
CHAIN = 16
VMEM_BYTES = 8 * 1024 * 1024


def sine_cosine(angle):
    turns = jnp.floor(angle * (2.0 / math.pi) + 0.5)
    rest = angle - turns * 1.5703125
    rest = rest - turns * 4.837512969970703125e-4
    rest = rest - turns * 7.549789948768648e-8
    square = rest * rest
    sine = rest + rest * square * (
        -1.6666654611e-1 + square * (8.3321608736e-3 + square * -1.9515295891e-4)
    )
    cosine = 1.0 - 0.5 * square + square * square * (
        4.166664568298827e-2 + square * (-1.388731625493765e-3 + square * 2.443315711809948e-5)
    )
    quadrant = turns.astype(jnp.int32) & 3
    swap = (quadrant & 1) == 1
    sine_out = jnp.where(swap, cosine, sine)
    cosine_out = jnp.where(swap, sine, cosine)
    sine_out = jnp.where(quadrant >= 2, -sine_out, sine_out)
    cosine_out = jnp.where((quadrant == 1) | (quadrant == 2), -cosine_out, cosine_out)
    return sine_out, cosine_out


def filtered_rows(echo_rows):
    rows = echo_rows.shape[0]
    lane = lax.broadcasted_iota(jnp.int32, echo_rows.shape, 1)
    inside = filter_taps[0] * echo_rows
    across = jnp.zeros_like(echo_rows)
    for lag in range(1, 8):
        moved = filter_taps[lag] * pltpu.roll(echo_rows, LANES - lag, 1)
        here = lane < LANES - lag
        inside = inside + jnp.where(here, moved, 0.0)
        across = across + jnp.where(here, 0.0, moved)
    return inside + pltpu.roll(across, rows - 1, 0)


def lane_lookup(row, lanes):
    return jnp.take_along_axis(row, lanes, axis=1, mode="promise_in_bounds")


def table_kernel(echo_hbm, offsets_hbm, look_hbm, table_ref, offsets_ref, look_ref, echo_ref, arrived):
    band = lax.axis_index("band")
    copies = [
        pltpu.make_async_copy(echo_hbm, echo_ref, arrived.at[0]),
        pltpu.make_async_copy(look_hbm, look_ref, arrived.at[1]),
    ]
    for slab in range(offsets_ref.shape[0]):
        block = pl.ds(pl.multiple_of((2 * slab + band) * LANES, LANES), LANES)
        copies.append(
            pltpu.make_async_copy(offsets_hbm.at[0, :, block], offsets_ref.at[slab], arrived.at[2 + slab])
        )
    for copy in copies:
        copy.start()
    lane = lax.broadcasted_iota(jnp.int32, (1, LANES), 1)
    phase_index = (lane * (5 + 2 * band)) & 63
    sine, cosine = sine_cosine(phase_index.astype(jnp.float32) * (math.pi / 32.0))
    copies[0].wait()
    filt = []
    for part in range(2):
        rows = echo_ref[part : part + 1].astype(jnp.float32).reshape(table_ref.shape[1], LANES)
        filt.append(filtered_rows(rows))
    table_ref[0] = cosine * filt[0] - sine * filt[1]
    table_ref[1] = sine * filt[0] + cosine * filt[1]
    for copy in copies[1:]:
        copy.wait()


def turn_kernel(delta_ref, look_ref, own_look_ref, turn_ref):
    band = lax.axis_index("band")
    for slab in range(own_look_ref.shape[0]):
        block = pl.ds(pl.multiple_of((2 * slab + band) * LANES, LANES), LANES)
        own_look_ref[slab : slab + 1] = look_ref[:, block]
    sine, cosine = sine_cosine(delta_ref[0] * own_look_ref[...])
    turn_ref[0] = cosine
    turn_ref[1] = sine


def pack(real, imag, words_ref):
    rows = real.shape[0]
    size = jnp.maximum(jnp.abs(real), jnp.abs(imag))
    lane = lax.broadcasted_iota(jnp.int32, size.shape, 1)
    row = lax.broadcasted_iota(jnp.int32, size.shape, 0)
    first_half = lane < LANES // 2
    tops = []
    for half in range(2):
        inside = first_half if half == 0 else jnp.logical_not(first_half)
        top = jnp.max(jnp.where(inside, size, 0.0), axis=1, keepdims=True)
        tops.append(jnp.where(top > 0.0, top, 1.0))
    shrink = jnp.where(first_half, 1.0 / tops[0], 1.0 / tops[1])
    real = jnp.floor(real * shrink * MOST + 0.5).astype(jnp.int32)
    imag = jnp.floor(imag * shrink * MOST + 0.5).astype(jnp.int32)
    words_ref[...] = (real << 16) | (imag & 0xFFFF)
    spread = jnp.where(lane == row, tops[0], 0.0) + jnp.where(lane == row + rows, tops[1], 0.0)
    return jnp.sum(spread, axis=0, keepdims=True)


def look_up(words_ref, tops, offsets):
    rows = words_ref.shape[0]
    lanes = offsets & (LANES - 1)
    high = offsets >> 7
    top = lane_lookup(jnp.broadcast_to(tops, offsets.shape), high + ((offsets & 64) * (rows // 64)))
    low = high & (CHAIN - 1)
    chains = [None] * (rows // CHAIN)
    for step in range(CHAIN):
        match = low == step
        for chain in range(len(chains)):
            row = chain * CHAIN + step
            here = lane_lookup(jnp.broadcast_to(words_ref[pl.ds(row, 1), :], offsets.shape), lanes)
            chains[chain] = here if step == 0 else jnp.where(match, here, chains[chain])
    found = chains[0]
    for chain in range(1, len(chains)):
        found = jnp.where(high >= chain * CHAIN, chains[chain], found)
    real = (found >> 16).astype(jnp.float32)
    imag = ((found << 16) >> 16).astype(jnp.float32)
    return real * (1.0 / MOST) * top, imag * (1.0 / MOST) * top


def terms_kernel(own_ref, other_ref, offsets_ref, look_ref, turn_ref, out_ref, words_ref):
    tops = pack(own_ref[0] + other_ref[0], own_ref[1] + other_ref[1], words_ref)
    for slab in range(offsets_ref.shape[0]):
        real, imag = look_up(words_ref, tops, offsets_ref[slab])
        cosine = turn_ref[0, slab : slab + 1]
        sine = turn_ref[1, slab : slab + 1]
        first = slab * CHUNK
        out_ref[first : first + ROWS_DEV, 0, :] = cosine * real - sine * imag
        out_ref[first + ROWS_DEV : first + 2 * ROWS_DEV, 0, :] = sine * real + cosine * imag
        out_ref[first + 2 * ROWS_DEV] = look_ref[slab : slab + 1]


def chunk_parts(terms_ref, part):
    first = part * ROWS_DEV
    starts = range(first, terms_ref.shape[0], CHUNK)
    return [terms_ref[start : start + ROWS_DEV, 0, :] for start in starts]


def image_kernel(terms_ref, image_ref, sums_ref):
    pulses = terms_ref.shape[0] // CHUNK
    copies = sums_ref.shape[0] // pulses
    reals = chunk_parts(terms_ref, 0)
    imags = chunk_parts(terms_ref, 1)
    looks = [terms_ref[p * CHUNK + 2 * ROWS_DEV] for p in range(pulses)]
    real = sum(reals[1:], reals[0])
    imag = sum(imags[1:], imags[0])
    image_ref[0] = real
    image_ref[1] = imag
    power = real * real + imag * imag
    power_sum = jnp.sum(jnp.sum(power, axis=0, keepdims=True), axis=1, keepdims=True)
    quart_sum = jnp.sum(jnp.sum(power * power, axis=0, keepdims=True), axis=1, keepdims=True)
    cross_rows, power_cross_rows = [], []
    for p in range(pulses):
        cross = imag * reals[p] - real * imags[p]
        cross_rows.append(looks[p] * jnp.sum(cross, axis=0, keepdims=True))
        power_cross_rows.append(looks[p] * jnp.sum(power * cross, axis=0, keepdims=True))
    cross_sums = jnp.sum(jnp.concatenate(cross_rows, axis=0), axis=1, keepdims=True)
    power_cross_sums = jnp.sum(jnp.concatenate(power_cross_rows, axis=0), axis=1, keepdims=True)
    lane = lax.broadcasted_iota(jnp.int32, (pulses, LANES), 1)
    sums = jnp.where(lane == 0, power_cross_sums, 0.0) + jnp.where(lane == 1, cross_sums, 0.0)
    sums = sums + jnp.where(lane == 2, power_sum, 0.0) + jnp.where(lane == 3, quart_sum, 0.0)
    for copy in range(copies):
        sums_ref[copy * pulses : (copy + 1) * pulses, 0, :] = sums


def join(own_ref, other_terms_ref, image_ref):
    band = lax.axis_index("band")
    for part in range(2):
        own = own_ref[part]
        parts = chunk_parts(other_terms_ref, part)
        other = sum(parts[1:], parts[0])
        image_ref[part, :, 0:LANES] = jnp.where(band == 0, own, other)
        image_ref[part, :, LANES:] = jnp.where(band == 0, other, own)


def gradient_kernel(own_ref, other_ref, sums_ref, gradient_ref, image_ref, *, pulses, npix):
    join(own_ref, other_ref, image_ref)
    totals = jnp.sum(sums_ref[:, 0, :], axis=0, keepdims=True)
    mean_power = totals[:, 2:3] / npix + power_floor
    quart = totals[:, 3:4] / npix
    gradient = 2.0 * totals[:, 0:1] / (mean_power * mean_power) - 2.0 * quart * totals[:, 1:2] / (
        mean_power * mean_power * mean_power
    )
    gradient_ref[...] = jnp.broadcast_to(math.sqrt(pulses / npix) * gradient, gradient_ref.shape)


SMEM, VMEM, HBM = (pl.BlockSpec(memory_space=space) for space in (pltpu.SMEM, pltpu.VMEM, pltpu.HBM))


def on_device(kernel, out, *operands, name, spaces=None, scratch=(), flops=0):
    return pl.pallas_call(
        kernel,
        out_shape=tuple(jax.ShapeDtypeStruct(shape, dtype) for shape, dtype in out),
        in_specs=spaces or [VMEM] * len(operands),
        out_specs=(VMEM,) * len(out),
        scratch_shapes=scratch,
        compiler_params=pltpu.CompilerParams(vmem_limit_bytes=VMEM_BYTES),
        cost_estimate=pl.CostEstimate(flops=flops, bytes_accessed=1 << 20, transcendentals=0),
        name=name,
    )(*operands)


def local(echo, offsets, delta, look):
    rows_dev, columns = offsets.shape[1:]
    bins = echo.shape[2]
    tiles = lax.axis_size("tile")
    pulses = lax.axis_size("pulse")
    bands = lax.axis_size("band")
    slabs = columns // (LANES * bands)
    npix = rows_dev * tiles * columns
    swap = [(0, 1), (1, 0)]
    f32, i32 = jnp.float32, jnp.int32
    table_shape = (2, bins // LANES, LANES)
    half_shape = (2, rows_dev, LANES)
    columns_shape = (slabs, LANES)

    inputs = (echo.reshape(2, bins), offsets, look)
    table, own_offsets, look = on_device(
        table_kernel,
        [(table_shape, f32), ((slabs, rows_dev, LANES), i32), ((1, columns), f32)],
        *(pltpu.with_memory_space_constraint(array, pltpu.HBM) for array in inputs),
        name="table", spaces=[HBM] * 3,
        scratch=[pltpu.VMEM((2, bins), echo.dtype), pltpu.SemaphoreType.DMA((2 + slabs,))],
    )
    other_table = lax.ppermute(table, "band", swap)
    own_look, turn = on_device(
        turn_kernel,
        [(columns_shape, f32), ((2,) + columns_shape, f32)],
        delta, look,
        name="turn", spaces=[SMEM, VMEM], flops=1 << 30,
    )
    (terms,) = on_device(
        terms_kernel,
        [((slabs * CHUNK, 1, LANES), f32)],
        table, other_table, own_offsets, own_look, turn,
        name="terms", scratch=[pltpu.VMEM(table_shape[1:], i32)],
    )
    terms = lax.all_to_all(terms, "pulse", 0, 0, tiled=True)
    other_terms = lax.ppermute(terms, "band", swap)
    half, sums = on_device(
        image_kernel, [(half_shape, f32), ((pulses * tiles * bands, 1, LANES), f32)], terms, name="image_sums"
    )
    sums = lax.all_to_all(sums, ("band", "tile", "pulse"), 0, 0, tiled=True)
    gradient, image = on_device(
        lambda *refs: gradient_kernel(*refs, pulses=pulses, npix=npix),
        [((1, LANES), f32), ((2, rows_dev, 2 * LANES), f32)],
        half, other_terms, sums, name="gradient",
    )
    return image, gradient[0, 0:1]


def solution(mesh):
    in_specs = (P(None, "pulse", "band"), P("pulse", "tile", None), P("pulse"), P("pulse", None))
    out_specs = (P(None, "tile", "pulse"), P("pulse"))
    return jax.shard_map(local, mesh=mesh, in_specs=in_specs, out_specs=out_specs, check_vma=False)
```

```python
import math

import jax
import jax.numpy as jnp
from jax import lax
from jax.experimental import pallas as pl
from jax.experimental.pallas import tpu as pltpu
from jax.sharding import PartitionSpec as P

filter_taps = (-0.0136, 0.0637, -0.1804, 0.6366, 0.6366, -0.1804, 0.0637, -0.0136)
power_floor = 1e-06

LANES = 128
ROWS_DEV = 8
CHUNK = 2 * ROWS_DEV + 1
MOST = 32767.0
CHAIN = 16
VMEM_BYTES = 8 * 1024 * 1024


def sine_cosine(angle):
    turns = jnp.floor(angle * (2.0 / math.pi) + 0.5)
    rest = angle - turns * 1.5703125
    rest = rest - turns * 4.837512969970703125e-4
    rest = rest - turns * 7.549789948768648e-8
    square = rest * rest
    sine = rest + rest * square * (
        -1.6666654611e-1 + square * (8.3321608736e-3 + square * -1.9515295891e-4)
    )
    cosine = 1.0 - 0.5 * square + square * square * (
        4.166664568298827e-2 + square * (-1.388731625493765e-3 + square * 2.443315711809948e-5)
    )
    quadrant = turns.astype(jnp.int32) & 3
    swap = (quadrant & 1) == 1
    sine_out = jnp.where(swap, cosine, sine)
    cosine_out = jnp.where(swap, sine, cosine)
    sine_out = jnp.where(quadrant >= 2, -sine_out, sine_out)
    cosine_out = jnp.where((quadrant == 1) | (quadrant == 2), -cosine_out, cosine_out)
    return sine_out, cosine_out


def filtered_rows(echo_rows):
    rows = echo_rows.shape[0]
    lane = lax.broadcasted_iota(jnp.int32, echo_rows.shape, 1)
    inside = filter_taps[0] * echo_rows
    across = jnp.zeros_like(echo_rows)
    for lag in range(1, 8):
        moved = filter_taps[lag] * pltpu.roll(echo_rows, LANES - lag, 1)
        here = lane < LANES - lag
        inside = inside + jnp.where(here, moved, 0.0)
        across = across + jnp.where(here, 0.0, moved)
    return inside + pltpu.roll(across, rows - 1, 0)


def send_order(peers):
    return list(range(peers))[::-1]


def lane_lookup(row, lanes):
    return jnp.take_along_axis(row, lanes, axis=1, mode="promise_in_bounds")


def table_kernel(echo_hbm, offsets_hbm, look_hbm, table_ref, offsets_ref, look_ref, echo_ref, arrived):
    band = lax.axis_index("band")
    copies = [
        pltpu.make_async_copy(echo_hbm, echo_ref, arrived.at[0]),
        pltpu.make_async_copy(look_hbm, look_ref, arrived.at[1]),
    ]
    for slab in range(offsets_ref.shape[0]):
        block = pl.ds(pl.multiple_of((2 * slab + band) * LANES, LANES), LANES)
        copies.append(
            pltpu.make_async_copy(offsets_hbm.at[0, :, block], offsets_ref.at[slab], arrived.at[2 + slab])
        )
    for copy in copies:
        copy.start()
    lane = lax.broadcasted_iota(jnp.int32, (1, LANES), 1)
    phase_index = (lane * (5 + 2 * band)) & 63
    sine, cosine = sine_cosine(phase_index.astype(jnp.float32) * (math.pi / 32.0))
    copies[0].wait()
    filt = []
    for part in range(2):
        rows = echo_ref[part : part + 1].astype(jnp.float32).reshape(table_ref.shape[1], LANES)
        filt.append(filtered_rows(rows))
    table_ref[0] = cosine * filt[0] - sine * filt[1]
    table_ref[1] = sine * filt[0] + cosine * filt[1]
    for copy in copies[1:]:
        copy.wait()


def turn_kernel(delta_ref, look_ref, own_look_ref, turn_ref):
    band = lax.axis_index("band")
    for slab in range(own_look_ref.shape[0]):
        block = pl.ds(pl.multiple_of((2 * slab + band) * LANES, LANES), LANES)
        own_look_ref[slab : slab + 1] = look_ref[:, block]
    sine, cosine = sine_cosine(delta_ref[0] * own_look_ref[...])
    turn_ref[0] = cosine
    turn_ref[1] = sine


def pack(real, imag, words_ref):
    rows = real.shape[0]
    size = jnp.maximum(jnp.abs(real), jnp.abs(imag))
    lane = lax.broadcasted_iota(jnp.int32, size.shape, 1)
    row = lax.broadcasted_iota(jnp.int32, size.shape, 0)
    first_half = lane < LANES // 2
    tops = []
    for half in range(2):
        inside = first_half if half == 0 else jnp.logical_not(first_half)
        top = jnp.max(jnp.where(inside, size, 0.0), axis=1, keepdims=True)
        tops.append(jnp.where(top > 0.0, top, 1.0))
    shrink = jnp.where(first_half, 1.0 / tops[0], 1.0 / tops[1])
    real = jnp.floor(real * shrink * MOST + 0.5).astype(jnp.int32)
    imag = jnp.floor(imag * shrink * MOST + 0.5).astype(jnp.int32)
    words_ref[...] = (real << 16) | (imag & 0xFFFF)
    spread = jnp.where(lane == row, tops[0], 0.0) + jnp.where(lane == row + rows, tops[1], 0.0)
    return jnp.sum(spread, axis=0, keepdims=True)


def look_up(words_ref, tops, offsets):
    rows = words_ref.shape[0]
    lanes = offsets & (LANES - 1)
    high = offsets >> 7
    top = lane_lookup(jnp.broadcast_to(tops, offsets.shape), high + ((offsets & 64) * (rows // 64)))
    low = high & (CHAIN - 1)
    chains = [None] * (rows // CHAIN)
    for step in range(CHAIN):
        match = low == step
        for chain in range(len(chains)):
            row = chain * CHAIN + step
            here = lane_lookup(jnp.broadcast_to(words_ref[pl.ds(row, 1), :], offsets.shape), lanes)
            chains[chain] = here if step == 0 else jnp.where(match, here, chains[chain])
    found = chains[0]
    for chain in range(1, len(chains)):
        found = jnp.where(high >= chain * CHAIN, chains[chain], found)
    real = (found >> 16).astype(jnp.float32)
    imag = ((found << 16) >> 16).astype(jnp.float32)
    return real * (1.0 / MOST) * top, imag * (1.0 / MOST) * top


def terms_kernel(own_ref, other_ref, offsets_ref, look_ref, turn_ref, out_ref, words_ref):
    tops = pack(own_ref[0] + other_ref[0], own_ref[1] + other_ref[1], words_ref)
    for place, slab in enumerate(send_order(offsets_ref.shape[0])):
        real, imag = look_up(words_ref, tops, offsets_ref[slab])
        cosine = turn_ref[0, slab : slab + 1]
        sine = turn_ref[1, slab : slab + 1]
        first = place * CHUNK
        out_ref[first : first + ROWS_DEV, 0, :] = cosine * real - sine * imag
        out_ref[first + ROWS_DEV : first + 2 * ROWS_DEV, 0, :] = sine * real + cosine * imag
        out_ref[first + 2 * ROWS_DEV] = look_ref[slab : slab + 1]


def chunk_parts(terms_ref, part):
    first = part * ROWS_DEV
    places = send_order(terms_ref.shape[0] // CHUNK)
    starts = [places.index(pulse) * CHUNK + first for pulse in range(len(places))]
    return [terms_ref[start : start + ROWS_DEV, 0, :] for start in starts]


def image_kernel(terms_ref, image_ref, sums_ref):
    pulses = terms_ref.shape[0] // CHUNK
    copies = sums_ref.shape[0] // pulses
    reals = chunk_parts(terms_ref, 0)
    imags = chunk_parts(terms_ref, 1)
    places = send_order(pulses)
    looks = [terms_ref[places.index(p) * CHUNK + 2 * ROWS_DEV] for p in range(pulses)]
    real = sum(reals[1:], reals[0])
    imag = sum(imags[1:], imags[0])
    image_ref[0] = real
    image_ref[1] = imag
    power = real * real + imag * imag
    power_sum = jnp.sum(jnp.sum(power, axis=0, keepdims=True), axis=1, keepdims=True)
    quart_sum = jnp.sum(jnp.sum(power * power, axis=0, keepdims=True), axis=1, keepdims=True)
    cross_rows, power_cross_rows = [], []
    for p in range(pulses):
        cross = imag * reals[p] - real * imags[p]
        cross_rows.append(looks[p] * jnp.sum(cross, axis=0, keepdims=True))
        power_cross_rows.append(looks[p] * jnp.sum(power * cross, axis=0, keepdims=True))
    cross_sums = jnp.sum(jnp.concatenate(cross_rows, axis=0), axis=1, keepdims=True)
    power_cross_sums = jnp.sum(jnp.concatenate(power_cross_rows, axis=0), axis=1, keepdims=True)
    lane = lax.broadcasted_iota(jnp.int32, (pulses, LANES), 1)
    sums = jnp.where(lane == 0, power_cross_sums, 0.0) + jnp.where(lane == 1, cross_sums, 0.0)
    sums = sums + jnp.where(lane == 2, power_sum, 0.0) + jnp.where(lane == 3, quart_sum, 0.0)
    for copy in range(copies):
        sums_ref[copy * pulses : (copy + 1) * pulses, 0, :] = sums


def join(own_ref, other_terms_ref, image_ref):
    band = lax.axis_index("band")
    for part in range(2):
        own = own_ref[part]
        parts = chunk_parts(other_terms_ref, part)
        other = sum(parts[1:], parts[0])
        image_ref[part, :, 0:LANES] = jnp.where(band == 0, own, other)
        image_ref[part, :, LANES:] = jnp.where(band == 0, other, own)


def gradient_kernel(own_ref, other_ref, sums_ref, gradient_ref, image_ref, *, pulses, npix):
    join(own_ref, other_ref, image_ref)
    totals = jnp.sum(sums_ref[:, 0, :], axis=0, keepdims=True)
    mean_power = totals[:, 2:3] / npix + power_floor
    quart = totals[:, 3:4] / npix
    gradient = 2.0 * totals[:, 0:1] / (mean_power * mean_power) - 2.0 * quart * totals[:, 1:2] / (
        mean_power * mean_power * mean_power
    )
    gradient_ref[...] = jnp.broadcast_to(math.sqrt(pulses / npix) * gradient, gradient_ref.shape)


SMEM, VMEM, HBM = (pl.BlockSpec(memory_space=space) for space in (pltpu.SMEM, pltpu.VMEM, pltpu.HBM))


def on_device(kernel, out, *operands, name, spaces=None, scratch=(), flops=0):
    return pl.pallas_call(
        kernel,
        out_shape=tuple(jax.ShapeDtypeStruct(shape, dtype) for shape, dtype in out),
        in_specs=spaces or [VMEM] * len(operands),
        out_specs=(VMEM,) * len(out),
        scratch_shapes=scratch,
        compiler_params=pltpu.CompilerParams(vmem_limit_bytes=VMEM_BYTES),
        cost_estimate=pl.CostEstimate(flops=flops, bytes_accessed=1 << 20, transcendentals=0),
        name=name,
    )(*operands)


def local(echo, offsets, delta, look):
    rows_dev, columns = offsets.shape[1:]
    bins = echo.shape[2]
    tiles = lax.axis_size("tile")
    pulses = lax.axis_size("pulse")
    bands = lax.axis_size("band")
    slabs = columns // (LANES * bands)
    npix = rows_dev * tiles * columns
    swap = [(0, 1), (1, 0)]
    f32, i32 = jnp.float32, jnp.int32
    table_shape = (2, bins // LANES, LANES)
    half_shape = (2, rows_dev, LANES)
    columns_shape = (slabs, LANES)

    inputs = (echo.reshape(2, bins), offsets, look)
    table, own_offsets, look = on_device(
        table_kernel,
        [(table_shape, f32), ((slabs, rows_dev, LANES), i32), ((1, columns), f32)],
        *(pltpu.with_memory_space_constraint(array, pltpu.HBM) for array in inputs),
        name="table", spaces=[HBM] * 3,
        scratch=[pltpu.VMEM((2, bins), echo.dtype), pltpu.SemaphoreType.DMA((2 + slabs,))],
    )
    other_table = lax.ppermute(table, "band", swap)
    own_look, turn = on_device(
        turn_kernel,
        [(columns_shape, f32), ((2,) + columns_shape, f32)],
        delta, look,
        name="turn", spaces=[SMEM, VMEM], flops=1 << 30,
    )
    (terms,) = on_device(
        terms_kernel,
        [((slabs * CHUNK, 1, LANES), f32)],
        table, other_table, own_offsets, own_look, turn,
        name="terms", scratch=[pltpu.VMEM(table_shape[1:], i32)],
    )
    terms = lax.all_to_all(
        terms, "pulse", 0, 0, tiled=True, axis_index_groups=[send_order(pulses)]
    )
    other_terms = lax.ppermute(terms, "band", swap)
    half, sums = on_device(
        image_kernel, [(half_shape, f32), ((pulses * tiles * bands, 1, LANES), f32)], terms, name="image_sums"
    )
    sums = lax.all_to_all(sums, ("band", "tile", "pulse"), 0, 0, tiled=True)
    gradient, image = on_device(
        lambda *refs: gradient_kernel(*refs, pulses=pulses, npix=npix),
        [((1, LANES), f32), ((2, rows_dev, 2 * LANES), f32)],
        half, other_terms, sums, name="gradient",
    )
    return image, gradient[0, 0:1]


def solution(mesh):
    in_specs = (P(None, "pulse", "band"), P("pulse", "tile", None), P("pulse"), P("pulse", None))
    out_specs = (P(None, "tile", "pulse"), P("pulse"))
    return jax.shard_map(local, mesh=mesh, in_specs=in_specs, out_specs=out_specs, check_vma=False)
```

```python
import math

import jax
import jax.numpy as jnp
from jax import lax
from jax.experimental import pallas as pl
from jax.experimental.pallas import tpu as pltpu
from jax.sharding import PartitionSpec as P

filter_taps = (-0.0136, 0.0637, -0.1804, 0.6366, 0.6366, -0.1804, 0.0637, -0.0136)
power_floor = 1e-06

LANES = 128
ROWS_DEV = 8
CHUNK = 2 * ROWS_DEV + 1
MOST = 32767.0
CHAIN = 16
VMEM_BYTES = 8 * 1024 * 1024


def sine_cosine(angle):
    turns = jnp.floor(angle * (2.0 / math.pi) + 0.5)
    rest = angle - turns * 1.5703125
    rest = rest - turns * 4.837512969970703125e-4
    rest = rest - turns * 7.549789948768648e-8
    square = rest * rest
    sine = rest + rest * square * (
        -1.6666654611e-1 + square * (8.3321608736e-3 + square * -1.9515295891e-4)
    )
    cosine = 1.0 - 0.5 * square + square * square * (
        4.166664568298827e-2 + square * (-1.388731625493765e-3 + square * 2.443315711809948e-5)
    )
    quadrant = turns.astype(jnp.int32) & 3
    swap = (quadrant & 1) == 1
    sine_out = jnp.where(swap, cosine, sine)
    cosine_out = jnp.where(swap, sine, cosine)
    sine_out = jnp.where(quadrant >= 2, -sine_out, sine_out)
    cosine_out = jnp.where((quadrant == 1) | (quadrant == 2), -cosine_out, cosine_out)
    return sine_out, cosine_out


def filtered_rows(echo_rows):
    rows = echo_rows.shape[0]
    lane = lax.broadcasted_iota(jnp.int32, echo_rows.shape, 1)
    inside = filter_taps[0] * echo_rows
    across = jnp.zeros_like(echo_rows)
    for lag in range(1, 8):
        moved = filter_taps[lag] * pltpu.roll(echo_rows, LANES - lag, 1)
        here = lane < LANES - lag
        inside = inside + jnp.where(here, moved, 0.0)
        across = across + jnp.where(here, 0.0, moved)
    return inside + pltpu.roll(across, rows - 1, 0)


def send_order(peers):
    return list(range(peers))[::-1]


def lane_lookup(row, lanes):
    return jnp.take_along_axis(row, lanes, axis=1, mode="promise_in_bounds")


def table_kernel(echo_hbm, offsets_hbm, look_hbm, table_ref, offsets_ref, look_ref, echo_ref, arrived):
    band = lax.axis_index("band")
    copies = [
        pltpu.make_async_copy(echo_hbm, echo_ref, arrived.at[0]),
        pltpu.make_async_copy(look_hbm, look_ref, arrived.at[1]),
    ]
    copies.append(pltpu.make_async_copy(offsets_hbm, offsets_ref, arrived.at[2]))
    for copy in copies:
        copy.start()
    lane = lax.broadcasted_iota(jnp.int32, (1, LANES), 1)
    phase_index = (lane * (5 + 2 * band)) & 63
    sine, cosine = sine_cosine(phase_index.astype(jnp.float32) * (math.pi / 32.0))
    copies[0].wait()
    filt = []
    for part in range(2):
        rows = echo_ref[part : part + 1].astype(jnp.float32).reshape(table_ref.shape[1], LANES)
        filt.append(filtered_rows(rows))
    table_ref[0] = cosine * filt[0] - sine * filt[1]
    table_ref[1] = sine * filt[0] + cosine * filt[1]
    for copy in copies[1:]:
        copy.wait()


def turn_kernel(delta_ref, look_ref, own_look_ref, turn_ref):
    band = lax.axis_index("band")
    for slab in range(own_look_ref.shape[0]):
        block = pl.ds(pl.multiple_of((2 * slab + band) * LANES, LANES), LANES)
        own_look_ref[slab : slab + 1] = look_ref[:, block]
    sine, cosine = sine_cosine(delta_ref[0] * own_look_ref[...])
    turn_ref[0] = cosine
    turn_ref[1] = sine


def pack(real, imag, words_ref):
    top = jnp.max(jnp.maximum(jnp.abs(real), jnp.abs(imag)), axis=0, keepdims=True)
    top = jnp.where(top > 0.0, top, 1.0)
    shrink = 1.0 / top
    real = jnp.floor(real * shrink * MOST + 0.5).astype(jnp.int32)
    imag = jnp.floor(imag * shrink * MOST + 0.5).astype(jnp.int32)
    words_ref[...] = (real << 16) | (imag & 0xFFFF)
    return top


def look_up(words_ref, tops, offsets):
    rows = words_ref.shape[0]
    lanes = offsets & (LANES - 1)
    high = offsets >> 7
    top = lane_lookup(jnp.broadcast_to(tops, offsets.shape), lanes)
    low = high & (CHAIN - 1)
    chains = [None] * (rows // CHAIN)
    for step in range(CHAIN):
        match = low == step
        for chain in range(len(chains)):
            row = chain * CHAIN + step
            here = lane_lookup(jnp.broadcast_to(words_ref[pl.ds(row, 1), :], offsets.shape), lanes)
            chains[chain] = here if step == 0 else jnp.where(match, here, chains[chain])
    found = chains[0]
    for chain in range(1, len(chains)):
        found = jnp.where(high >= chain * CHAIN, chains[chain], found)
    real = (found >> 16).astype(jnp.float32)
    imag = ((found << 16) >> 16).astype(jnp.float32)
    return real * (1.0 / MOST) * top, imag * (1.0 / MOST) * top


def terms_kernel(own_ref, other_ref, offsets_ref, look_ref, turn_ref, out_ref, words_ref):
    tops = pack(own_ref[0] + other_ref[0], own_ref[1] + other_ref[1], words_ref)
    band = lax.axis_index("band")
    for place, slab in enumerate(send_order(look_ref.shape[0])):
        block = pl.ds(pl.multiple_of((2 * slab + band) * LANES, LANES), LANES)
        real, imag = look_up(words_ref, tops, offsets_ref[0, :, block])
        cosine = turn_ref[0, slab : slab + 1]
        sine = turn_ref[1, slab : slab + 1]
        first = place * CHUNK
        out_ref[first : first + ROWS_DEV, 0, :] = cosine * real - sine * imag
        out_ref[first + ROWS_DEV : first + 2 * ROWS_DEV, 0, :] = sine * real + cosine * imag
        out_ref[first + 2 * ROWS_DEV] = look_ref[slab : slab + 1]


def chunk_parts(terms_ref, part):
    first = part * ROWS_DEV
    places = send_order(terms_ref.shape[0] // CHUNK)
    starts = [places.index(pulse) * CHUNK + first for pulse in range(len(places))]
    return [terms_ref[start : start + ROWS_DEV, 0, :] for start in starts]


def image_kernel(terms_ref, image_ref, sums_ref):
    pulses = terms_ref.shape[0] // CHUNK
    copies = sums_ref.shape[0] // pulses
    reals = chunk_parts(terms_ref, 0)
    imags = chunk_parts(terms_ref, 1)
    places = send_order(pulses)
    looks = [terms_ref[places.index(p) * CHUNK + 2 * ROWS_DEV] for p in range(pulses)]
    real = sum(reals[1:], reals[0])
    imag = sum(imags[1:], imags[0])
    image_ref[0] = real
    image_ref[1] = imag
    power = real * real + imag * imag
    power_sum = jnp.sum(jnp.sum(power, axis=0, keepdims=True), axis=1, keepdims=True)
    quart_sum = jnp.sum(jnp.sum(power * power, axis=0, keepdims=True), axis=1, keepdims=True)
    cross_rows, power_cross_rows = [], []
    for p in range(pulses):
        cross = imag * reals[p] - real * imags[p]
        cross_rows.append(looks[p] * jnp.sum(cross, axis=0, keepdims=True))
        power_cross_rows.append(looks[p] * jnp.sum(power * cross, axis=0, keepdims=True))
    cross_sums = jnp.sum(jnp.concatenate(cross_rows, axis=0), axis=1, keepdims=True)
    power_cross_sums = jnp.sum(jnp.concatenate(power_cross_rows, axis=0), axis=1, keepdims=True)
    lane = lax.broadcasted_iota(jnp.int32, (pulses, LANES), 1)
    sums = jnp.where(lane == 0, power_cross_sums, 0.0) + jnp.where(lane == 1, cross_sums, 0.0)
    sums = sums + jnp.where(lane == 2, power_sum, 0.0) + jnp.where(lane == 3, quart_sum, 0.0)
    for copy in range(copies):
        sums_ref[copy * pulses : (copy + 1) * pulses] = sums


def join(own_ref, other_terms_ref, image_ref):
    band = lax.axis_index("band")
    for part in range(2):
        own = own_ref[part]
        parts = chunk_parts(other_terms_ref, part)
        other = sum(parts[1:], parts[0])
        image_ref[part, :, 0:LANES] = jnp.where(band == 0, own, other)
        image_ref[part, :, LANES:] = jnp.where(band == 0, other, own)


def gradient_kernel(own_ref, other_ref, sums_ref, gradient_ref, image_ref, *, pulses, npix):
    join(own_ref, other_ref, image_ref)
    totals = jnp.sum(sums_ref[...], axis=0, keepdims=True)
    mean_power = totals[:, 2:3] / npix + power_floor
    quart = totals[:, 3:4] / npix
    gradient = 2.0 * totals[:, 0:1] / (mean_power * mean_power) - 2.0 * quart * totals[:, 1:2] / (
        mean_power * mean_power * mean_power
    )
    gradient_ref[...] = jnp.broadcast_to(math.sqrt(pulses / npix) * gradient, gradient_ref.shape)


SMEM, VMEM, HBM = (pl.BlockSpec(memory_space=space) for space in (pltpu.SMEM, pltpu.VMEM, pltpu.HBM))


def on_device(kernel, out, *operands, name, spaces=None, scratch=(), flops=0):
    return pl.pallas_call(
        kernel,
        out_shape=tuple(jax.ShapeDtypeStruct(shape, dtype) for shape, dtype in out),
        in_specs=spaces or [VMEM] * len(operands),
        out_specs=(VMEM,) * len(out),
        scratch_shapes=scratch,
        compiler_params=pltpu.CompilerParams(vmem_limit_bytes=VMEM_BYTES),
        cost_estimate=pl.CostEstimate(flops=flops, bytes_accessed=1 << 20, transcendentals=0),
        name=name,
    )(*operands)


def local(echo, offsets, delta, look):
    rows_dev, columns = offsets.shape[1:]
    bins = echo.shape[2]
    tiles = lax.axis_size("tile")
    pulses = lax.axis_size("pulse")
    bands = lax.axis_size("band")
    slabs = columns // (LANES * bands)
    npix = rows_dev * tiles * columns
    swap = [(0, 1), (1, 0)]
    f32, i32 = jnp.float32, jnp.int32
    table_shape = (2, bins // LANES, LANES)
    half_shape = (2, rows_dev, LANES)
    columns_shape = (slabs, LANES)

    inputs = (echo.reshape(2, bins), offsets, look)
    table, own_offsets, look = on_device(
        table_kernel,
        [(table_shape, f32), ((1, rows_dev, columns), i32), ((1, columns), f32)],
        *(pltpu.with_memory_space_constraint(array, pltpu.HBM) for array in inputs),
        name="table", spaces=[HBM] * 3,
        scratch=[pltpu.VMEM((2, bins), echo.dtype), pltpu.SemaphoreType.DMA((3,))],
    )
    other_table = lax.ppermute(table, "band", swap)
    own_look, turn = on_device(
        turn_kernel,
        [(columns_shape, f32), ((2,) + columns_shape, f32)],
        delta, look,
        name="turn", spaces=[SMEM, VMEM], flops=1 << 30,
    )
    (terms,) = on_device(
        terms_kernel,
        [((slabs * CHUNK, 1, LANES), f32)],
        table, other_table, own_offsets, own_look, turn,
        name="terms", scratch=[pltpu.VMEM(table_shape[1:], i32)],
    )
    terms = lax.all_to_all(
        terms, "pulse", 0, 0, tiled=True, axis_index_groups=[send_order(pulses)]
    )
    other_terms = lax.ppermute(terms, "band", swap)
    half, sums = on_device(
        image_kernel, [(half_shape, f32), ((pulses * tiles * bands, LANES), f32)], terms, name="image_sums"
    )
    sums = lax.all_to_all(sums, ("band", "tile", "pulse"), 0, 0, tiled=True)
    gradient, image = on_device(
        lambda *refs: gradient_kernel(*refs, pulses=pulses, npix=npix),
        [((1, LANES), f32), ((2, rows_dev, 2 * LANES), f32)],
        half, other_terms, sums, name="gradient",
    )
    return image, gradient[0, 0:1]


def solution(mesh):
    in_specs = (P(None, "pulse", "band"), P("pulse", "tile", None), P("pulse"), P("pulse", None))
    out_specs = (P(None, "tile", "pulse"), P("pulse"))
    return jax.shard_map(local, mesh=mesh, in_specs=in_specs, out_specs=out_specs, check_vma=False)
```

```python
import math

import jax
import jax.numpy as jnp
from jax import lax
from jax.experimental import pallas as pl
from jax.experimental.pallas import tpu as pltpu
from jax.sharding import PartitionSpec as P

filter_taps = (-0.0136, 0.0637, -0.1804, 0.6366, 0.6366, -0.1804, 0.0637, -0.0136)
power_floor = 1e-06

LANES = 128
ROWS_DEV = 8
CHUNK = 2 * ROWS_DEV + 1
MOST = 32767.0
CHAIN = 16
VMEM_BYTES = 8 * 1024 * 1024


def sine_cosine(angle):
    turns = jnp.floor(angle * (2.0 / math.pi) + 0.5)
    rest = angle - turns * 1.5703125
    rest = rest - turns * 4.837512969970703125e-4
    rest = rest - turns * 7.549789948768648e-8
    square = rest * rest
    sine = rest + rest * square * (
        -1.6666654611e-1 + square * (8.3321608736e-3 + square * -1.9515295891e-4)
    )
    cosine = 1.0 - 0.5 * square + square * square * (
        4.166664568298827e-2 + square * (-1.388731625493765e-3 + square * 2.443315711809948e-5)
    )
    quadrant = turns.astype(jnp.int32) & 3
    swap = (quadrant & 1) == 1
    sine_out = jnp.where(swap, cosine, sine)
    cosine_out = jnp.where(swap, sine, cosine)
    sine_out = jnp.where(quadrant >= 2, -sine_out, sine_out)
    cosine_out = jnp.where((quadrant == 1) | (quadrant == 2), -cosine_out, cosine_out)
    return sine_out, cosine_out


def filtered_rows(echo_rows):
    rows = echo_rows.shape[0]
    lane = lax.broadcasted_iota(jnp.int32, echo_rows.shape, 1)
    inside = filter_taps[0] * echo_rows
    across = jnp.zeros_like(echo_rows)
    for lag in range(1, 8):
        moved = filter_taps[lag] * pltpu.roll(echo_rows, LANES - lag, 1)
        here = lane < LANES - lag
        inside = inside + jnp.where(here, moved, 0.0)
        across = across + jnp.where(here, 0.0, moved)
    return inside + pltpu.roll(across, rows - 1, 0)


def send_order(peers):
    return list(range(peers))[::-1]


def lane_lookup(row, lanes):
    return jnp.take_along_axis(row, lanes, axis=1, mode="promise_in_bounds")


def table_kernel(echo_hbm, offsets_hbm, look_hbm, table_ref, offsets_ref, look_ref, echo_ref, arrived):
    band = lax.axis_index("band")
    copies = [
        pltpu.make_async_copy(echo_hbm, echo_ref, arrived.at[0]),
        pltpu.make_async_copy(look_hbm, look_ref, arrived.at[1]),
    ]
    copies.append(pltpu.make_async_copy(offsets_hbm, offsets_ref, arrived.at[2]))
    for copy in copies:
        copy.start()
    lane = lax.broadcasted_iota(jnp.int32, (1, LANES), 1)
    phase_index = (lane * (5 + 2 * band)) & 63
    sine, cosine = sine_cosine(phase_index.astype(jnp.float32) * (math.pi / 32.0))
    copies[0].wait()
    filt = []
    for part in range(2):
        rows = echo_ref[part : part + 1].astype(jnp.float32).reshape(table_ref.shape[1], LANES)
        filt.append(filtered_rows(rows))
    table_ref[0] = cosine * filt[0] - sine * filt[1]
    table_ref[1] = sine * filt[0] + cosine * filt[1]
    for copy in copies[1:]:
        copy.wait()


def turn_kernel(delta_ref, look_ref, own_look_ref, turn_ref):
    band = lax.axis_index("band")
    for slab in range(own_look_ref.shape[0]):
        block = pl.ds(pl.multiple_of((2 * slab + band) * LANES, LANES), LANES)
        own_look_ref[slab : slab + 1] = look_ref[:, block]
    sine, cosine = sine_cosine(delta_ref[0] * own_look_ref[...])
    turn_ref[0] = cosine
    turn_ref[1] = sine


def pack(real, imag, words_ref):
    top = jnp.max(jnp.maximum(jnp.abs(real), jnp.abs(imag)), axis=0, keepdims=True)
    top = jnp.where(top > 0.0, top, 1.0)
    shrink = 1.0 / top
    real = jnp.floor(real * shrink * MOST + 0.5).astype(jnp.int32)
    imag = jnp.floor(imag * shrink * MOST + 0.5).astype(jnp.int32)
    words_ref[...] = (real << 16) | (imag & 0xFFFF)
    return top


def look_up(words_ref, tops, offsets):
    rows = words_ref.shape[0]
    lanes = offsets & (LANES - 1)
    high = offsets >> 7
    top = lane_lookup(jnp.broadcast_to(tops, offsets.shape), lanes)
    low = high & (CHAIN - 1)
    chains = [None] * (rows // CHAIN)
    for step in range(CHAIN):
        match = low == step
        for chain in range(len(chains)):
            row = chain * CHAIN + step
            here = lane_lookup(jnp.broadcast_to(words_ref[pl.ds(row, 1), :], offsets.shape), lanes)
            chains[chain] = here if step == 0 else jnp.where(match, here, chains[chain])
    found = chains[0]
    for chain in range(1, len(chains)):
        found = jnp.where(high >= chain * CHAIN, chains[chain], found)
    real = (found >> 16).astype(jnp.float32)
    imag = ((found << 16) >> 16).astype(jnp.float32)
    return real * (1.0 / MOST) * top, imag * (1.0 / MOST) * top


def terms_kernel(own_ref, other_ref, offsets_ref, look_ref, turn_ref, out_ref, words_ref):
    tops = pack(own_ref[0] + other_ref[0], own_ref[1] + other_ref[1], words_ref)
    band = lax.axis_index("band")
    for place, slab in enumerate(send_order(look_ref.shape[0])):
        block = pl.ds(pl.multiple_of((2 * slab + band) * LANES, LANES), LANES)
        real, imag = look_up(words_ref, tops, offsets_ref[0, :, block])
        cosine = turn_ref[0, slab : slab + 1]
        sine = turn_ref[1, slab : slab + 1]
        first = place * CHUNK
        out_ref[first : first + ROWS_DEV] = cosine * real - sine * imag
        out_ref[first + ROWS_DEV : first + 2 * ROWS_DEV] = sine * real + cosine * imag
        out_ref[first + 2 * ROWS_DEV : first + CHUNK] = look_ref[slab : slab + 1]


def chunk_parts(terms_ref, part):
    first = part * ROWS_DEV
    places = send_order(terms_ref.shape[0] // CHUNK)
    starts = [places.index(pulse) * CHUNK + first for pulse in range(len(places))]
    return [terms_ref[start : start + ROWS_DEV] for start in starts]


def image_kernel(terms_ref, image_ref, sums_ref):
    pulses = terms_ref.shape[0] // CHUNK
    copies = sums_ref.shape[0] // pulses
    reals = chunk_parts(terms_ref, 0)
    imags = chunk_parts(terms_ref, 1)
    places = send_order(pulses)
    firsts = [places.index(p) * CHUNK + 2 * ROWS_DEV for p in range(pulses)]
    looks = [terms_ref[first : first + 1] for first in firsts]
    real = sum(reals[1:], reals[0])
    imag = sum(imags[1:], imags[0])
    image_ref[0] = real
    image_ref[1] = imag
    power = real * real + imag * imag
    power_sum = jnp.sum(jnp.sum(power, axis=0, keepdims=True), axis=1, keepdims=True)
    quart_sum = jnp.sum(jnp.sum(power * power, axis=0, keepdims=True), axis=1, keepdims=True)
    cross_rows, power_cross_rows = [], []
    for p in range(pulses):
        cross = imag * reals[p] - real * imags[p]
        cross_rows.append(looks[p] * jnp.sum(cross, axis=0, keepdims=True))
        power_cross_rows.append(looks[p] * jnp.sum(power * cross, axis=0, keepdims=True))
    cross_sums = jnp.sum(jnp.concatenate(cross_rows, axis=0), axis=1, keepdims=True)
    power_cross_sums = jnp.sum(jnp.concatenate(power_cross_rows, axis=0), axis=1, keepdims=True)
    lane = lax.broadcasted_iota(jnp.int32, (pulses, LANES), 1)
    sums = jnp.where(lane == 0, power_cross_sums, 0.0) + jnp.where(lane == 1, cross_sums, 0.0)
    sums = sums + jnp.where(lane == 2, power_sum, 0.0) + jnp.where(lane == 3, quart_sum, 0.0)
    for copy in range(copies):
        sums_ref[copy * pulses : (copy + 1) * pulses] = sums


def join(own_ref, other_terms_ref, image_ref):
    band = lax.axis_index("band")
    for part in range(2):
        own = own_ref[part]
        parts = chunk_parts(other_terms_ref, part)
        other = sum(parts[1:], parts[0])
        image_ref[part, :, 0:LANES] = jnp.where(band == 0, own, other)
        image_ref[part, :, LANES:] = jnp.where(band == 0, other, own)


def gradient_kernel(own_ref, other_ref, sums_ref, gradient_ref, image_ref, *, pulses, npix):
    join(own_ref, other_ref, image_ref)
    totals = jnp.sum(sums_ref[...], axis=0, keepdims=True)
    mean_power = totals[:, 2:3] / npix + power_floor
    quart = totals[:, 3:4] / npix
    gradient = 2.0 * totals[:, 0:1] / (mean_power * mean_power) - 2.0 * quart * totals[:, 1:2] / (
        mean_power * mean_power * mean_power
    )
    gradient_ref[...] = jnp.broadcast_to(math.sqrt(pulses / npix) * gradient, gradient_ref.shape)


SMEM, VMEM, HBM = (pl.BlockSpec(memory_space=space) for space in (pltpu.SMEM, pltpu.VMEM, pltpu.HBM))


def on_device(kernel, out, *operands, name, spaces=None, scratch=(), flops=0):
    return pl.pallas_call(
        kernel,
        out_shape=tuple(jax.ShapeDtypeStruct(shape, dtype) for shape, dtype in out),
        in_specs=spaces or [VMEM] * len(operands),
        out_specs=(VMEM,) * len(out),
        scratch_shapes=scratch,
        compiler_params=pltpu.CompilerParams(vmem_limit_bytes=VMEM_BYTES),
        cost_estimate=pl.CostEstimate(flops=flops, bytes_accessed=1 << 20, transcendentals=0),
        name=name,
    )(*operands)


def local(echo, offsets, delta, look):
    rows_dev, columns = offsets.shape[1:]
    bins = echo.shape[2]
    tiles = lax.axis_size("tile")
    pulses = lax.axis_size("pulse")
    bands = lax.axis_size("band")
    slabs = columns // (LANES * bands)
    npix = rows_dev * tiles * columns
    swap = [(0, 1), (1, 0)]
    f32, i32 = jnp.float32, jnp.int32
    table_shape = (2, bins // LANES, LANES)
    half_shape = (2, rows_dev, LANES)
    columns_shape = (slabs, LANES)

    inputs = (echo.reshape(2, bins), offsets, look)
    table, own_offsets, look = on_device(
        table_kernel,
        [(table_shape, f32), ((1, rows_dev, columns), i32), ((1, columns), f32)],
        *(pltpu.with_memory_space_constraint(array, pltpu.HBM) for array in inputs),
        name="table", spaces=[HBM] * 3,
        scratch=[pltpu.VMEM((2, bins), echo.dtype), pltpu.SemaphoreType.DMA((3,))],
    )
    other_table = lax.ppermute(table, "band", swap)
    own_look, turn = on_device(
        turn_kernel,
        [(columns_shape, f32), ((2,) + columns_shape, f32)],
        delta, look,
        name="turn", spaces=[SMEM, VMEM], flops=1 << 30,
    )
    (terms,) = on_device(
        terms_kernel,
        [((slabs * CHUNK, LANES), f32)],
        table, other_table, own_offsets, own_look, turn,
        name="terms", scratch=[pltpu.VMEM(table_shape[1:], i32)],
    )
    terms = lax.all_to_all(
        terms.reshape(-1, 1, LANES), "pulse", 0, 0, tiled=True, axis_index_groups=[send_order(pulses)]
    ).reshape(-1, LANES)
    other_terms = lax.ppermute(terms, "band", swap)
    half, sums = on_device(
        image_kernel, [(half_shape, f32), ((pulses * tiles * bands, LANES), f32)], terms, name="image_sums"
    )
    sums = lax.all_to_all(sums, ("band", "tile", "pulse"), 0, 0, tiled=True)
    gradient, image = on_device(
        lambda *refs: gradient_kernel(*refs, pulses=pulses, npix=npix),
        [((1, LANES), f32), ((2, rows_dev, 2 * LANES), f32)],
        half, other_terms, sums, name="gradient",
    )
    return image, gradient[0, 0:1]


def solution(mesh):
    in_specs = (P(None, "pulse", "band"), P("pulse", "tile", None), P("pulse"), P("pulse", None))
    out_specs = (P(None, "tile", "pulse"), P("pulse"))
    return jax.shard_map(local, mesh=mesh, in_specs=in_specs, out_specs=out_specs, check_vma=False)
```

```python
import math

import jax
import jax.numpy as jnp
from jax import lax
from jax.experimental import pallas as pl
from jax.experimental.pallas import tpu as pltpu
from jax.sharding import PartitionSpec as P

filter_taps = (-0.0136, 0.0637, -0.1804, 0.6366, 0.6366, -0.1804, 0.0637, -0.0136)
power_floor = 1e-06

LANES = 128
ROWS_DEV = 8
CHUNK = 2 * ROWS_DEV + 1
MOST = 32767.0
CHAIN = 16
VMEM_BYTES = 8 * 1024 * 1024


def sine_cosine(angle):
    turns = jnp.floor(angle * (2.0 / math.pi) + 0.5)
    rest = angle - turns * 1.5703125
    rest = rest - turns * 4.837512969970703125e-4
    rest = rest - turns * 7.549789948768648e-8
    square = rest * rest
    sine = rest + rest * square * (
        -1.6666654611e-1 + square * (8.3321608736e-3 + square * -1.9515295891e-4)
    )
    cosine = 1.0 - 0.5 * square + square * square * (
        4.166664568298827e-2 + square * (-1.388731625493765e-3 + square * 2.443315711809948e-5)
    )
    quadrant = turns.astype(jnp.int32) & 3
    swap = (quadrant & 1) == 1
    sine_out = jnp.where(swap, cosine, sine)
    cosine_out = jnp.where(swap, sine, cosine)
    sine_out = jnp.where(quadrant >= 2, -sine_out, sine_out)
    cosine_out = jnp.where((quadrant == 1) | (quadrant == 2), -cosine_out, cosine_out)
    return sine_out, cosine_out


def filtered_rows(echo_rows):
    rows = echo_rows.shape[0]
    lane = lax.broadcasted_iota(jnp.int32, echo_rows.shape, 1)
    inside = filter_taps[0] * echo_rows
    across = jnp.zeros_like(echo_rows)
    for lag in range(1, 8):
        moved = filter_taps[lag] * pltpu.roll(echo_rows, LANES - lag, 1)
        here = lane < LANES - lag
        inside = inside + jnp.where(here, moved, 0.0)
        across = across + jnp.where(here, 0.0, moved)
    return inside + pltpu.roll(across, rows - 1, 0)


def send_order(peers):
    return list(range(peers))[::-1]


def lane_lookup(row, lanes):
    return jnp.take_along_axis(row, lanes, axis=1, mode="promise_in_bounds")


def table_kernel(echo_hbm, offsets_hbm, look_hbm, table_ref, offsets_ref, look_ref, echo_ref, arrived):
    band = lax.axis_index("band")
    copies = [
        pltpu.make_async_copy(echo_hbm, echo_ref, arrived.at[0]),
        pltpu.make_async_copy(look_hbm, look_ref, arrived.at[1]),
    ]
    copies.append(pltpu.make_async_copy(offsets_hbm, offsets_ref, arrived.at[2]))
    for copy in copies:
        copy.start()
    lane = lax.broadcasted_iota(jnp.int32, (1, LANES), 1)
    phase_index = (lane * (5 + 2 * band)) & 63
    sine, cosine = sine_cosine(phase_index.astype(jnp.float32) * (math.pi / 32.0))
    copies[0].wait()
    rows = table_ref.shape[1]
    both = filtered_rows(echo_ref[...].astype(jnp.float32).reshape(2 * rows, LANES))
    filt = both[:rows], both[rows:]
    table_ref[0] = cosine * filt[0] - sine * filt[1]
    table_ref[1] = sine * filt[0] + cosine * filt[1]
    for copy in copies[1:]:
        copy.wait()


def turn_kernel(delta_ref, look_ref, own_look_ref, turn_ref):
    band = lax.axis_index("band")
    for slab in range(own_look_ref.shape[0]):
        block = pl.ds(pl.multiple_of((2 * slab + band) * LANES, LANES), LANES)
        own_look_ref[slab : slab + 1] = look_ref[:, block]
    sine, cosine = sine_cosine(delta_ref[0] * own_look_ref[...])
    turn_ref[0] = cosine
    turn_ref[1] = sine


def pack(real, imag, words_ref):
    top = jnp.max(jnp.maximum(jnp.abs(real), jnp.abs(imag)), axis=0, keepdims=True)
    top = jnp.where(top > 0.0, top, 1.0)
    shrink = 1.0 / top
    real = jnp.floor(real * shrink * MOST + 0.5).astype(jnp.int32)
    imag = jnp.floor(imag * shrink * MOST + 0.5).astype(jnp.int32)
    words_ref[...] = (real << 16) | (imag & 0xFFFF)
    return top


def look_up(words_ref, tops, offsets):
    rows = words_ref.shape[0]
    lanes = offsets & (LANES - 1)
    high = offsets >> 7
    top = lane_lookup(jnp.broadcast_to(tops, offsets.shape), lanes)
    low = high & (CHAIN - 1)
    chains = [None] * (rows // CHAIN)
    for step in range(CHAIN):
        match = low == step
        for chain in range(len(chains)):
            row = chain * CHAIN + step
            here = lane_lookup(jnp.broadcast_to(words_ref[pl.ds(row, 1), :], offsets.shape), lanes)
            chains[chain] = here if step == 0 else jnp.where(match, here, chains[chain])
    found = chains[0]
    for chain in range(1, len(chains)):
        found = jnp.where(high >= chain * CHAIN, chains[chain], found)
    real = (found >> 16).astype(jnp.float32)
    imag = ((found << 16) >> 16).astype(jnp.float32)
    return real * (1.0 / MOST) * top, imag * (1.0 / MOST) * top


def terms_kernel(own_ref, other_ref, offsets_ref, look_ref, turn_ref, out_ref, words_ref):
    tops = pack(own_ref[0] + other_ref[0], own_ref[1] + other_ref[1], words_ref)
    band = lax.axis_index("band")
    for place, slab in enumerate(send_order(look_ref.shape[0])):
        block = pl.ds(pl.multiple_of((2 * slab + band) * LANES, LANES), LANES)
        real, imag = look_up(words_ref, tops, offsets_ref[0, :, block])
        cosine = turn_ref[0, slab : slab + 1]
        sine = turn_ref[1, slab : slab + 1]
        first = place * CHUNK
        out_ref[first : first + ROWS_DEV] = cosine * real - sine * imag
        out_ref[first + ROWS_DEV : first + 2 * ROWS_DEV] = sine * real + cosine * imag
        out_ref[first + 2 * ROWS_DEV : first + CHUNK] = look_ref[slab : slab + 1]


def chunk_parts(terms_ref, part):
    first = part * ROWS_DEV
    places = send_order(terms_ref.shape[0] // CHUNK)
    starts = [places.index(pulse) * CHUNK + first for pulse in range(len(places))]
    return [terms_ref[start : start + ROWS_DEV] for start in starts]


def image_kernel(terms_ref, image_ref, sums_ref):
    pulses = terms_ref.shape[0] // CHUNK
    copies = sums_ref.shape[0] // pulses
    reals = chunk_parts(terms_ref, 0)
    imags = chunk_parts(terms_ref, 1)
    places = send_order(pulses)
    firsts = [places.index(p) * CHUNK + 2 * ROWS_DEV for p in range(pulses)]
    looks = [terms_ref[first : first + 1] for first in firsts]
    real = sum(reals[1:], reals[0])
    imag = sum(imags[1:], imags[0])
    image_ref[0] = real
    image_ref[1] = imag
    power = real * real + imag * imag
    power_sum = jnp.sum(jnp.sum(power, axis=0, keepdims=True), axis=1, keepdims=True)
    quart_sum = jnp.sum(jnp.sum(power * power, axis=0, keepdims=True), axis=1, keepdims=True)
    cross_rows, power_cross_rows = [], []
    for p in range(pulses):
        cross = imag * reals[p] - real * imags[p]
        cross_rows.append(looks[p] * jnp.sum(cross, axis=0, keepdims=True))
        power_cross_rows.append(looks[p] * jnp.sum(power * cross, axis=0, keepdims=True))
    cross_sums = jnp.sum(jnp.concatenate(cross_rows, axis=0), axis=1, keepdims=True)
    power_cross_sums = jnp.sum(jnp.concatenate(power_cross_rows, axis=0), axis=1, keepdims=True)
    lane = lax.broadcasted_iota(jnp.int32, (pulses, LANES), 1)
    sums = jnp.where(lane == 0, power_cross_sums, 0.0) + jnp.where(lane == 1, cross_sums, 0.0)
    sums = sums + jnp.where(lane == 2, power_sum, 0.0) + jnp.where(lane == 3, quart_sum, 0.0)
    for copy in range(copies):
        sums_ref[copy * pulses : (copy + 1) * pulses] = sums


def join(own_ref, other_terms_ref, image_ref):
    band = lax.axis_index("band")
    for part in range(2):
        own = own_ref[part]
        parts = chunk_parts(other_terms_ref, part)
        other = sum(parts[1:], parts[0])
        image_ref[part, :, 0:LANES] = jnp.where(band == 0, own, other)
        image_ref[part, :, LANES:] = jnp.where(band == 0, other, own)


def gradient_kernel(own_ref, other_ref, sums_ref, gradient_ref, image_ref, *, pulses, npix):
    join(own_ref, other_ref, image_ref)
    totals = jnp.sum(sums_ref[...], axis=0, keepdims=True)
    mean_power = totals[:, 2:3] / npix + power_floor
    quart = totals[:, 3:4] / npix
    gradient = 2.0 * totals[:, 0:1] / (mean_power * mean_power) - 2.0 * quart * totals[:, 1:2] / (
        mean_power * mean_power * mean_power
    )
    gradient_ref[...] = jnp.broadcast_to(math.sqrt(pulses / npix) * gradient, gradient_ref.shape)


SMEM, VMEM, HBM = (pl.BlockSpec(memory_space=space) for space in (pltpu.SMEM, pltpu.VMEM, pltpu.HBM))


def on_device(kernel, out, *operands, name, spaces=None, scratch=(), flops=0):
    return pl.pallas_call(
        kernel,
        out_shape=tuple(jax.ShapeDtypeStruct(shape, dtype) for shape, dtype in out),
        in_specs=spaces or [VMEM] * len(operands),
        out_specs=(VMEM,) * len(out),
        scratch_shapes=scratch,
        compiler_params=pltpu.CompilerParams(vmem_limit_bytes=VMEM_BYTES),
        cost_estimate=pl.CostEstimate(flops=flops, bytes_accessed=1 << 20, transcendentals=0),
        name=name,
    )(*operands)


def local(echo, offsets, delta, look):
    rows_dev, columns = offsets.shape[1:]
    bins = echo.shape[2]
    tiles = lax.axis_size("tile")
    pulses = lax.axis_size("pulse")
    bands = lax.axis_size("band")
    slabs = columns // (LANES * bands)
    npix = rows_dev * tiles * columns
    swap = [(0, 1), (1, 0)]
    f32, i32 = jnp.float32, jnp.int32
    table_shape = (2, bins // LANES, LANES)
    half_shape = (2, rows_dev, LANES)
    columns_shape = (slabs, LANES)

    inputs = (echo.reshape(2, bins), offsets, look)
    table, own_offsets, look = on_device(
        table_kernel,
        [(table_shape, f32), ((1, rows_dev, columns), i32), ((1, columns), f32)],
        *(pltpu.with_memory_space_constraint(array, pltpu.HBM) for array in inputs),
        name="table", spaces=[HBM] * 3,
        scratch=[pltpu.VMEM((2, bins), echo.dtype), pltpu.SemaphoreType.DMA((3,))],
    )
    other_table = lax.ppermute(table, "band", swap)
    own_look, turn = on_device(
        turn_kernel,
        [(columns_shape, f32), ((2,) + columns_shape, f32)],
        delta, look,
        name="turn", spaces=[SMEM, VMEM], flops=1 << 30,
    )
    (terms,) = on_device(
        terms_kernel,
        [((slabs * CHUNK, LANES), f32)],
        table, other_table, own_offsets, own_look, turn,
        name="terms", scratch=[pltpu.VMEM(table_shape[1:], i32)],
    )
    terms = lax.all_to_all(
        terms.reshape(-1, 1, LANES), "pulse", 0, 0, tiled=True, axis_index_groups=[send_order(pulses)]
    ).reshape(-1, LANES)
    other_terms = lax.ppermute(terms, "band", swap)
    half, sums = on_device(
        image_kernel, [(half_shape, f32), ((pulses * tiles * bands, LANES), f32)], terms, name="image_sums"
    )
    sums = lax.all_to_all(sums, ("band", "tile", "pulse"), 0, 0, tiled=True)
    gradient, image = on_device(
        lambda *refs: gradient_kernel(*refs, pulses=pulses, npix=npix),
        [((1, LANES), f32), ((2, rows_dev, 2 * LANES), f32)],
        half, other_terms, sums, name="gradient",
    )
    return image, gradient[0, 0:1]


def solution(mesh):
    in_specs = (P(None, "pulse", "band"), P("pulse", "tile", None), P("pulse"), P("pulse", None))
    out_specs = (P(None, "tile", "pulse"), P("pulse"))
    return jax.shard_map(local, mesh=mesh, in_specs=in_specs, out_specs=out_specs, check_vma=False)
```
